256 devices in a mesh: dp: 32 (over y, x, core), mp: 8 (over z).
Axes of the slice: x: 4, y: 4, z: 8, core: 2. Of those that a mesh axis runs over, the one named last changes fastest.
Arguments:
- token_keys: bfloat16 [4096, 25600], P('dp', 'mp'), may hold values from -6 to 6
- token_grads: bfloat16 [4096, 5120], P('dp', 'mp'), may hold values from -6 to 6
- prompt_ids: int32 [4096], P('dp'), may hold values from 0 to 511, never falling along the last dimension, each value on 1 to 32 neighbouring positions
- key_weight: bfloat16 [25600, 1024], P('mp'), may hold values from -0.0390625 to 0.0390625
- grad_weight: bfloat16 [5120, 1024], P('mp'), may hold values from -0.078125 to 0.078125
- hidden_bias: float32 [1024], replicated, may hold values from -3 to 3
- gate_vector: float32 [1024], replicated, may hold values from -0.375 to 0.375
- grad_output: bfloat16 [1024, 5120], P(None, 'mp'), may hold values from -0.1875 to 0.1875
- down_weight: bfloat16 [25600, 5120], P('mp', 'dp'), may hold values from -0.0390625 to 0.0390625
- locality_bank: bfloat16 [320, 25600], P(None, 'mp'), may hold values from -6 to 6
- locality_ids: int32 [256], replicated, may hold values from 0 to 319
Outputs:
- locality_out: bfloat16 [256, 5120], P('mp', 'dp')
The draws below stay inside these ranges and needn't reach their ends.
Inputs may be any that keep to these rules, and one draw needn't show every extreme that they name: prompt_ids never fall along the tokens; every prompt has 1 to 32 tokens and some prompt has exactly 32.
All inputs are finite; a program needn't handle non-finite values.
Results may differ from the reference program's by a relative error of at most 0.024.
Values may be sent and summed in bfloat16 or wider, within the bound.
A program may use at most 128 MiB of HBM per device.

```python
import math
import jax
import jax.numpy as jnp
import numpy as np
from jax import lax

D = 5120
FF = 25600
R = 1024
MOST = 32
LROWS = 256
BANK = 320
TOKENS = 4096
PROMPTS = 512


def set_ends(array, stream_key, smallest, high):
    longest = array.shape.index(max(array.shape))
    spots = []
    for shift in (0, 1):
        where = [jax.random.randint(jax.random.fold_in(stream_key, axis), (), 0, length) for axis, length in enumerate(array.shape)]
        where[longest] = (where[longest] + shift) % array.shape[longest]
        spots.append(tuple(where))
    return array.at[spots[0]].set(smallest).at[spots[1]].set(high)


def shard_levels(stream_key, dims, cuts, least, high):
    def one(position, parts):
        draws = jax.random.uniform(jax.random.fold_in(jax.random.fold_in(stream_key, 6), position), (parts,), jnp.float32, least / len(cuts), high / len(cuts))
        return jnp.repeat(jnp.exp(draws), dims[position] // parts).reshape((-1,) + (1,) * (len(dims) - position - 1))

    factor_of = one(*cuts[0])
    for cut in cuts[1:]:
        factor_of = factor_of * one(*cut)
    return factor_of


def split_up(number_of, total, reach, lean):
    weights = [(1 << 20) // math.isqrt(standing ** lean) + 1 for standing in range(2, number_of + 1)]
    spare, given = total - reach - (number_of - 1), [1] * (number_of - 1)
    while spare > 0:
        candidates = [i for i in range(number_of - 1) if given[i] < reach]
        mass, remaining = sum([weights[i] for i in candidates]), spare
        for i in candidates:
            extra = min(reach - given[i], max(1, remaining * weights[i] // mass), spare)
            given[i] = given[i] + extra
            spare = spare - extra
    return np.array([reach] + given)


def ragged(stream_key, amount, total, limit, slope):
    if amount == 2:
        one = jax.random.randint(stream_key, (), max(1, total - limit), min(limit, total - 1) + 1)
        return jnp.stack([one, total - one])
    lengths = jnp.asarray(split_up(amount, total, limit, slope), jnp.int32)
    couples = (amount - 1) // 2
    source_of, taker = lengths[1:1 + 2 * couples:2], lengths[2:2 + 2 * couples:2]
    margin = jnp.minimum(source_of - 1, limit - taker)
    shifted = jax.random.randint(jax.random.fold_in(stream_key, 1), (couples,), 0, 1 << 20) % (margin + 1)
    lengths = lengths.at[1:1 + 2 * couples:2].set(source_of - shifted).at[2:2 + 2 * couples:2].set(taker + shifted)
    return lengths[jax.random.permutation(jax.random.fold_in(stream_key, 2), amount)]


def bell_draw(stream_key, extent, scale, bound, pieces=(), kind=jnp.bfloat16):
    result = jax.random.normal(stream_key, extent, jnp.float32) * scale
    if len(pieces) > 0:
        result = shard_levels(stream_key, extent, pieces, -0.22, 0.18) * result
    return jnp.clip(result, min=-bound, max=bound).astype(kind)


def setup_inputs(seed: int = 0) -> dict:
    seeds = jax.random.split(jax.random.key(seed), 12)
    token_keys = bell_draw(seeds[0], (TOKENS, FF), 1.0, 6.0, ((0, 32), (1, 8)))
    token_grads = bell_draw(seeds[1], (TOKENS, D), 1.0, 6.0, ((0, 32), (1, 8)))
    prompt_ids = jnp.searchsorted(jnp.cumsum(ragged(seeds[2], PROMPTS, TOKENS, MOST, 2)), jnp.arange(TOKENS), side="right").astype(jnp.int32)
    key_weight = bell_draw(seeds[3], (FF, R), FF ** -0.5, 0.0390625, ((0, 8),))
    grad_weight = bell_draw(seeds[4], (D, R), D ** -0.5, 0.078125, ((0, 8),))
    hidden_bias = bell_draw(seeds[5], (R,), 0.5, 3.0, (), jnp.float32)
    gate_vector = bell_draw(seeds[6], (R,), (R // 4) ** -0.5, 0.375, (), jnp.float32)
    grad_output = bell_draw(seeds[7], (R, D), R ** -0.5, 0.1875, ((1, 8),))
    down_weight = bell_draw(seeds[8], (FF, D), FF ** -0.5, 0.0390625, ((0, 8), (1, 32)))
    locality_bank = bell_draw(seeds[9], (BANK, FF), 1.0, 6.0, ((1, 8),))
    locality_ids = set_ends(jax.random.randint(seeds[10], (LROWS,), 0, BANK), jax.random.fold_in(seeds[10], 1), 0, BANK - 1).astype(jnp.int32)
    return dict(token_keys=token_keys, token_grads=token_grads, prompt_ids=prompt_ids, key_weight=key_weight, grad_weight=grad_weight, hidden_bias=hidden_bias, gate_vector=gate_vector, grad_output=grad_output, down_weight=down_weight, locality_bank=locality_bank, locality_ids=locality_ids)


def split_product(scores, grads):
    upper = scores.astype(jnp.bfloat16)
    lower = (scores - upper.astype(jnp.float32)).astype(jnp.bfloat16)
    first = jnp.dot(upper, grads, preferred_element_type=jnp.float32)
    return first + jnp.dot(lower, grads, preferred_element_type=jnp.float32)

def reference(token_keys, token_grads, prompt_ids, key_weight, grad_weight, hidden_bias, gate_vector, grad_output, down_weight, locality_bank, locality_ids):
    pre_act = jnp.dot(token_keys, key_weight, preferred_element_type=jnp.float32)
    pre_act = pre_act + jnp.dot(token_grads, grad_weight, preferred_element_type=jnp.float32) + hidden_bias
    hidden = jax.nn.relu(pre_act).astype(jnp.bfloat16)
    onehot = (prompt_ids[:, None] == jnp.arange(PROMPTS, dtype=jnp.int32)[None, :]).astype(jnp.float32)
    counts = lax.optimization_barrier(jnp.sum(onehot, axis=0))
    token_count = jnp.dot(onehot, counts, precision=lax.Precision.HIGHEST)
    gate_value = 2.0 * jax.nn.sigmoid(lax.optimization_barrier(jnp.sum(hidden.astype(jnp.float32) * gate_vector[None, :], axis=1)))
    weighting = gate_value / token_count
    pseudo_keys = (token_keys.astype(jnp.float32) * weighting[:, None]).astype(jnp.bfloat16)
    pseudo_grads = (token_grads.astype(jnp.float32) + jnp.dot(hidden, grad_output, preferred_element_type=jnp.float32)).astype(jnp.bfloat16)
    locality = jnp.take(locality_bank, locality_ids, axis=0)
    base_term = jnp.dot(locality, down_weight, preferred_element_type=jnp.float32)
    scores = lax.dot_general(locality, pseudo_keys, (((1,), (1,)), ((), ())), preferred_element_type=jnp.float32)
    spread = split_product(scores, pseudo_grads)
    factor_shift = 4.0 / jnp.sqrt(jnp.float32(FF) * jnp.float32(TOKENS))
    return (base_term + factor_shift * spread).astype(jnp.bfloat16)
```

```python
import jax
import jax.numpy as jnp
from jax import lax
from jax.sharding import PartitionSpec as P

FF = 25600


def local(
    token_keys,
    token_grads,
    prompt_ids,
    key_weight,
    grad_weight,
    hidden_bias,
    gate_vector,
    grad_output,
    down_weight,
    locality_bank,
    locality_ids,
):
    n_dp, n_mp = lax.axis_size("dp"), lax.axis_size("mp")
    rows = locality_ids.shape[0]
    locality = jnp.take(locality_bank, locality_ids, axis=0)
    base_term = jnp.dot(locality, down_weight, preferred_element_type=jnp.float32)
    scores = lax.dot_general(
        token_keys, locality, (((1,), (1,)), ((), ())), preferred_element_type=jnp.float32
    )
    partial_value = jnp.dot(token_keys, key_weight, preferred_element_type=jnp.float32)
    partial_value = partial_value + jnp.dot(
        token_grads, grad_weight, preferred_element_type=jnp.float32
    )
    both = jnp.concatenate([partial_value, scores], axis=1).astype(jnp.bfloat16)
    both = lax.psum(both, "mp")
    width = partial_value.shape[1]
    pre_act = both[:, :width].astype(jnp.float32)
    scores = both[:, width:]
    hidden = jax.nn.relu(pre_act + hidden_bias).astype(jnp.bfloat16)
    left = lax.ppermute(prompt_ids, "dp", [(i, (i + 1) % n_dp) for i in range(n_dp)])
    right = lax.ppermute(prompt_ids, "dp", [(i, (i - 1) % n_dp) for i in range(n_dp)])
    near = jnp.concatenate([left, prompt_ids, right])
    token_count = jnp.sum((prompt_ids[:, None] == near[None, :]).astype(jnp.float32), axis=1)
    gate_value = 2.0 * jax.nn.sigmoid(
        jnp.sum(hidden.astype(jnp.float32) * gate_vector[None, :], axis=1)
    )
    weighting = gate_value / token_count
    pseudo_grads = token_grads.astype(jnp.float32) + jnp.dot(
        hidden, grad_output, preferred_element_type=jnp.float32
    )
    weighted = (pseudo_grads * weighting[:, None]).astype(jnp.bfloat16)
    spread = lax.dot_general(
        scores, weighted, (((0,), (0,)), ((), ())), preferred_element_type=jnp.float32
    ).astype(jnp.bfloat16)
    cols = n_dp // n_mp
    high, wide = rows // n_mp, spread.shape[1] // cols
    blocks = spread.reshape(n_mp, high, cols, wide).transpose(0, 2, 1, 3).reshape(n_dp, high, wide)
    mine = lax.psum_scatter(blocks, "dp", scatter_dimension=0, tiled=True)[0]
    pairs = []
    for d in range(n_dp):
        for m in range(n_mp):
            pairs.append((d * n_mp + m, (m * cols + d % cols) * n_mp + d // cols))
    mine = lax.ppermute(mine, ("dp", "mp"), pairs).astype(jnp.float32)
    base = lax.psum_scatter(
        base_term.astype(jnp.bfloat16), "mp", scatter_dimension=0, tiled=True
    ).astype(jnp.float32)
    token_total = n_dp * token_keys.shape[0]
    factor_shift = 4.0 / jnp.sqrt(jnp.float32(FF) * jnp.float32(token_total))
    return (base + factor_shift * mine).astype(jnp.bfloat16)


def solution(mesh):
    placed = (
        P("dp", "mp"),
        P("dp", "mp"),
        P("dp"),
        P("mp", None),
        P("mp", None),
        P(),
        P(),
        P(None, "mp"),
        P("mp", "dp"),
        P(None, "mp"),
        P(),
    )
    return jax.shard_map(
        local, mesh=mesh, in_specs=placed, out_specs=P("mp", "dp"), check_vma=False
    )
```

```python
import jax
import jax.numpy as jnp
from jax import lax
from jax.experimental import pallas as pl
from jax.experimental.pallas import tpu as pltpu
from jax.sharding import PartitionSpec as P

MESH = pl.DeviceIdType.MESH
F32, BF16 = jnp.float32, jnp.bfloat16
NZ, NX, NY, NCHIP = 8, 4, 4, 16
TOK, KEYS, GRADS, HID, ROWS, BANK, COLS = 128, 3200, 640, 1024, 256, 320, 160
TB = TOK // NZ
RB = ROWS // NCHIP
HALF = HID // 2
WIDE = 384
CH = 256
NCH = HID // CH
OB = ROWS // NZ
SCALE = 4.0 / 10240.0

TN = (((0,), (0,)), ((), ()))
NT = (((1,), (1,)), ((), ()))


def kernel(
    tk_h, tg_h, ids_h, kw_h, gw_h, bias_h, gate_h, go_h, dw_h, bank_h, lids_h,
    out_ref,
    tk, tg, ids, kw, gw, bias, gate, go, dw, bank, lids,
    near, pbuf, rz, bbuf, br, hid, swt, uh_tx, uh_rx, uh_sum, uh_rs, ug_tx, ug_rx, ug_sum, ug_rs,
    uz_tx, uz, mm, ftx, frx,
    lsem, kwsem, rz_s, rz_r, b_s, b_r, i_s, i_r, a_s, a_r, c_s, c_r, x_s, x_r, z_s, z_r, f_s, f_r,
):
    d, m = lax.axis_index("dp"), lax.axis_index("mp")
    c = lax.rem(d, 2)
    q = lax.div(d, 2)
    y, x = lax.div(q, NX), lax.rem(q, NX)
    sibling = (d + 1 - 2 * c, m)

    def zdev(k):
        return (d, lax.rem(m + k, NZ))

    def chip(k):
        ky, kx = divmod(k, NX)
        return lax.rem(y + ky, NY) * NX + lax.rem(x + kx, NX)

    def rows_of(chip_index):
        return pl.ds(pl.multiple_of(lax.rem(chip_index + NCHIP // 2, NCHIP) * RB, RB), RB)

    def remote(src, dst, s, r, dev):
        pltpu.make_async_remote_copy(
            src_ref=src, dst_ref=dst, send_sem=s, recv_sem=r, device_id=dev, device_id_type=MESH
        ).start()

    def await_bytes(buf, sem):
        pltpu.make_async_copy(buf, buf, sem).wait()

    core_rows = pl.ds(pl.multiple_of(c * HALF, HALF), HALF)
    loads = dict(
        tk=(tk_h, tk), bank=(bank_h, bank), lids=(lids_h, lids), tg=(tg_h, tg), gw=(gw_h, gw),
        ids=(ids_h, ids), bias=(bias_h, bias), gate=(gate_h, gate),
        dw=(dw_h, dw), go=(go_h.at[core_rows], go),
    )
    number = {name: i for i, name in enumerate(loads)}

    def load(name):
        src, dst = loads[name]
        return pltpu.make_async_copy(src, dst, lsem.at[number[name]])

    def load_kw(ch):
        return pltpu.make_async_copy(kw_h.at[:, pl.ds(ch * CH, CH)], kw.at[ch], kwsem.at[ch])

    for name in ("tk", "bank", "lids", "ids", "tg", "gw"):
        load(name).start()
    for ch in range(NCH):
        load_kw(ch).start()
    for name in ("bias", "gate", "dw", "go"):
        load(name).start()

    barrier = pltpu.get_barrier_semaphore()
    beside = [lax.rem(d + 1, 2 * NCHIP), lax.rem(d + 2 * NCHIP - 1, 2 * NCHIP)]
    target = lax.rem(lax.div(d, 4) + NZ // 2, NZ)
    greet = [sibling] + [(e, m) for e in beside]
    greet += [zdev(k) for k in range(1, NZ)]
    greet += [(chip(k) * 2 + c, m) for k in range(1, NCHIP)]
    greet += [(4 * lax.rem(m + NZ // 2, NZ) + s, lax.div(d, 4)) for s in range(4)]
    for dev in greet:
        pl.semaphore_signal(barrier, inc=1, device_id=dev, device_id_type=MESH)

    load("lids").wait()
    ids_row = lids[...].astype(F32)
    pick_t = (
        lax.broadcasted_iota(jnp.int32, (BANK, ROWS), 0).astype(F32) == ids_row
    ).astype(F32).astype(BF16)
    load("tk").wait()
    load("bank").wait()
    bank_scores = lax.dot_general(tk[...], bank[...], NT, preferred_element_type=F32).astype(BF16)
    pbuf[NCH] = jnp.dot(bank_scores, pick_t, preferred_element_type=F32).astype(BF16)
    load("tg").wait()
    load("gw").wait()

    def partial_sum(ch):
        load_kw(ch).wait()
        value = jnp.dot(tk[...], kw[ch], preferred_element_type=F32)
        value = value + jnp.dot(
            tg[...], gw[:, ch * CH:(ch + 1) * CH], preferred_element_type=F32
        )
        pbuf[ch] = value.astype(BF16)

    def send_partial(ch):
        for k in range(1, NZ):
            to = lax.rem(m + k, NZ)
            rows = pl.ds(pl.multiple_of(to * TB, TB), TB)
            remote(pbuf.at[ch, rows], rz.at[ch, k - 1], rz_s.at[ch], rz_r.at[ch], (d, to))

    partial_sum(0)
    load("ids").wait()
    pl.semaphore_wait(barrier, len(greet))
    send_partial(0)
    send_partial(NCH)
    for i, e in enumerate(beside):
        remote(ids, near.at[i], i_s.at[i], i_r.at[i], (e, m))
    for ch in range(1, NCH):
        partial_sum(ch)
        send_partial(ch)

    load("dw").wait()
    square = lax.broadcasted_iota(jnp.int32, (ROWS, ROWS), 0) == lax.broadcasted_iota(
        jnp.int32, (ROWS, ROWS), 1
    )
    ids_col = jnp.sum(jnp.where(square, jnp.broadcast_to(ids_row, (ROWS, ROWS)), 0.0), axis=1, keepdims=True)
    pick = (
        lax.broadcasted_iota(jnp.int32, (ROWS, BANK), 1).astype(F32) == ids_col
    ).astype(F32).astype(BF16)
    bank_down = lax.dot_general(bank[...], dw[...], NT, preferred_element_type=F32).astype(BF16)
    bbuf[...] = jnp.dot(pick, bank_down, preferred_element_type=F32).astype(BF16)
    for k in range(1, NZ):
        to = lax.rem(m + k, NZ)
        remote(
            bbuf.at[pl.ds(pl.multiple_of(to * OB, OB), OB)], br.at[k - 1], b_s.at[0], b_r.at[0], (d, to)
        )

    own_ids = ids[...].astype(F32)
    wanted = lax.broadcasted_iota(jnp.int32, (TB, TOK), 1) == (
        lax.broadcasted_iota(jnp.int32, (TB, TOK), 0) + m * TB
    )
    ids_here = jnp.sum(jnp.where(wanted, jnp.broadcast_to(own_ids, (TB, TOK)), 0.0), axis=1, keepdims=True)
    count = jnp.sum((ids_here == own_ids).astype(F32), axis=1, keepdims=True)
    for i in range(2):
        pltpu.make_async_copy(ids, near.at[i], i_r.at[i]).wait()
        count = count + jnp.sum((ids_here == near[i].astype(F32)).astype(F32), axis=1, keepdims=True)

    load("bias").wait()
    load("gate").wait()
    mine = pl.ds(pl.multiple_of(m * TB, TB), TB)

    def summed(ch):
        await_bytes(rz.at[ch], rz_r.at[ch])
        value = pbuf[ch, mine].astype(F32)
        for k in range(NZ - 1):
            value = value + rz[ch, k].astype(F32)
        return value

    gated = jnp.zeros((TB, 1), F32)
    for ch in range(NCH):
        cut = slice(ch * CH, (ch + 1) * CH)
        hidden = jnp.maximum(summed(ch) + bias[:, cut], 0.0).astype(BF16)
        hid[:, cut] = hidden
        gated = gated + jnp.sum(hidden.astype(F32) * gate[:, cut], axis=1, keepdims=True)
    weight = 2.0 / ((1.0 + jnp.exp(-gated)) * count)
    sw = (summed(NCH) * weight).astype(BF16)
    swt[mine] = sw
    for k in range(1, NZ):
        remote(swt.at[mine], swt.at[mine], a_s.at[0], a_r.at[0], zdev(k))

    def half(core):
        return pl.ds(pl.multiple_of(core * HALF, HALF), HALF)

    uh_tx[...] = lax.dot_general(sw, hid[:, half(1 - c)], TN, preferred_element_type=F32).astype(BF16)
    remote(uh_tx, uh_rx, c_s.at[0], c_r.at[0], sibling)
    own = lax.dot_general(sw, hid[:, half(c)], TN, preferred_element_type=F32)
    await_bytes(uh_rx, c_r.at[0])
    uh_sum[...] = (own + uh_rx[...].astype(F32)).astype(BF16)
    for k in range(1, NCHIP):
        to = chip(k)
        remote(uh_sum.at[rows_of(to)], uh_rs.at[k - 1], x_s.at[0], x_r.at[0], (to * 2 + c, m))

    def window(core):
        return pl.ds(pl.multiple_of(core * 256, 256), WIDE)

    await_bytes(swt.at[pl.ds(0, TOK - TB)], a_r.at[0])
    scores = swt[...]
    ug_tx[...] = lax.dot_general(scores, tg[:, window(1 - c)], TN, preferred_element_type=F32).astype(BF16)
    remote(ug_tx, ug_rx, c_s.at[1], c_r.at[1], sibling)
    own = lax.dot_general(scores, tg[:, window(c)], TN, preferred_element_type=F32)
    await_bytes(ug_rx, c_r.at[1])
    ug_sum[...] = (own + ug_rx[...].astype(F32)).astype(BF16)
    for k in range(1, NCHIP):
        to = chip(k)
        remote(ug_sum.at[rows_of(to)], ug_rs.at[k - 1], x_s.at[1], x_r.at[1], (to * 2 + c, m))

    await_bytes(uh_rs, x_r.at[0])
    value = uh_sum[rows_of(q)].astype(F32)
    for k in range(NCHIP - 1):
        value = value + uh_rs[k].astype(F32)
    uz_tx[...] = value.astype(BF16)
    for k in range(1, NZ):
        remote(uz_tx, uz.at[k - 1], z_s.at[0], z_r.at[0], zdev(k))

    await_bytes(ug_rs, x_r.at[1])
    grads_part = ug_sum[rows_of(q)].astype(F32)
    for k in range(NCHIP - 1):
        grads_part = grads_part + ug_rs[k].astype(F32)
    lane = lax.broadcasted_iota(jnp.int32, (RB, WIDE), 1)
    grads_part = jnp.where(lane >= c * 128, grads_part, 0.0)

    load("go").wait()
    await_bytes(uz, z_r.at[0])
    for k in range(NZ - 1):
        value = value + uz[k].astype(F32)
    mm[...] = jnp.dot(value.astype(BF16), go[...], preferred_element_type=F32)
    mm[:, window(c)] = mm[:, window(c)] + grads_part
    ftx[...] = mm[...].astype(BF16)
    slot = lax.rem(d, 4)
    for j in range(4):
        remote(ftx.at[:, pl.ds(128 * j, 256)], frx.at[slot], f_s.at[0], f_r.at[0], (4 * m + j, target))

    await_bytes(br, b_r.at[0])
    base = bbuf[pl.ds(pl.multiple_of(m * OB, OB), OB)].astype(F32)
    for k in range(NZ - 1):
        base = base + br[k].astype(F32)
    await_bytes(frx, f_r.at[0])
    spread = jnp.concatenate(
        [frx[0].astype(F32) + frx[1].astype(F32), frx[2].astype(F32) + frx[3].astype(F32)], axis=0
    )
    spread = pltpu.roll(spread, lax.rem(256 - 32 * slot, 256), 1)
    out_ref[...] = (base + SCALE * spread[:, :COLS]).astype(BF16)

    for ch in range(NCH + 1):
        await_bytes(rz.at[ch], rz_s.at[ch])
    await_bytes(br, b_s.at[0])
    for i in range(2):
        pltpu.make_async_copy(ids, near.at[i], i_s.at[i]).wait()
    await_bytes(swt.at[pl.ds(0, TOK - TB)], a_s.at[0])
    await_bytes(uh_rx, c_s.at[0])
    await_bytes(ug_rx, c_s.at[1])
    await_bytes(uh_rs, x_s.at[0])
    await_bytes(ug_rs, x_s.at[1])
    await_bytes(uz, z_s.at[0])
    await_bytes(frx, f_s.at[0])


def local(
    token_keys, token_grads, prompt_ids, key_weight, grad_weight, hidden_bias, gate_vector, grad_output,
    down_weight, locality_bank, locality_ids,
):
    vm = pltpu.VMEM
    dma = pltpu.SemaphoreType.DMA
    scratch = [
        vm((TOK, KEYS), BF16), vm((TOK, GRADS), BF16), vm((1, TOK), jnp.int32),
        vm((NCH, KEYS, CH), BF16), vm((GRADS, HID), BF16), vm((1, HID), F32), vm((1, HID), F32),
        vm((HALF, GRADS), BF16), vm((COLS, KEYS), BF16), vm((BANK, KEYS), BF16), vm((1, ROWS), jnp.int32),
        vm((2, 1, TOK), jnp.int32),
        vm((NCH + 1, TOK, CH), BF16), vm((NCH + 1, NZ - 1, TB, CH), BF16),
        vm((ROWS, COLS), BF16), vm((NZ - 1, OB, COLS), BF16),
        vm((TB, HID), BF16), vm((TOK, ROWS), BF16),
        vm((ROWS, HALF), BF16), vm((ROWS, HALF), BF16), vm((ROWS, HALF), BF16),
        vm((NCHIP - 1, RB, HALF), BF16),
        vm((ROWS, WIDE), BF16), vm((ROWS, WIDE), BF16), vm((ROWS, WIDE), BF16),
        vm((NCHIP - 1, RB, WIDE), BF16),
        vm((RB, HALF), BF16), vm((NZ - 1, RB, HALF), BF16),
        vm((RB, GRADS), F32), vm((RB, GRADS), BF16), vm((4, RB, 256), BF16),
        dma((10,)), dma((NCH,)), dma((NCH + 1,)), dma((NCH + 1,)), dma((1,)), dma((1,)), dma((2,)), dma((2,)),
        dma((1,)), dma((1,)), dma((2,)), dma((2,)), dma((2,)), dma((2,)), dma((1,)), dma((1,)), dma((1,)), dma((1,)),
    ]
    any_spec = pl.BlockSpec(memory_space=pl.ANY)
    return pl.pallas_call(
        kernel,
        out_shape=jax.ShapeDtypeStruct((OB, COLS), BF16),
        in_specs=[any_spec] * 11,
        out_specs=pl.BlockSpec(memory_space=pltpu.VMEM),
        scratch_shapes=scratch,
        compiler_params=pltpu.CompilerParams(
            collective_id=0, has_side_effects=True, vmem_limit_bytes=60 * 1024 * 1024
        ),
        cost_estimate=pl.CostEstimate(flops=2_000_000_000, bytes_accessed=14_000_000, transcendentals=16),
    )(
        token_keys, token_grads, prompt_ids.reshape(1, TOK), key_weight, grad_weight,
        hidden_bias.reshape(1, HID), gate_vector.reshape(1, HID), grad_output, down_weight.T, locality_bank,
        locality_ids.reshape(1, ROWS),
    )


def solution(mesh):
    placed = (
        P("dp", "mp"), P("dp", "mp"), P("dp"), P("mp", None), P("mp", None), P(), P(), P(None, "mp"),
        P("mp", "dp"), P(None, "mp"), P(),
    )
    return jax.shard_map(
        local, mesh=mesh, in_specs=placed, out_specs=P("mp", "dp"), check_vma=False
    )
```

```python
import jax
import jax.numpy as jnp
from jax import lax
from jax.experimental import pallas as pl
from jax.experimental.pallas import tpu as pltpu
from jax.sharding import PartitionSpec as P

MESH = pl.DeviceIdType.MESH
F32, BF16 = jnp.float32, jnp.bfloat16
NZ, NX, NY, NCHIP = 8, 4, 4, 16
TOK, KEYS, GRADS, HID, ROWS, BANK, COLS = 128, 3200, 640, 1024, 256, 320, 160
TB = TOK // NZ
RB = ROWS // NCHIP
HALF = HID // 2
WIDE = 384
CH = 256
NCH = HID // CH
OB = ROWS // NZ
SCALE = 4.0 / 10240.0

TN = (((0,), (0,)), ((), ()))
NT = (((1,), (1,)), ((), ()))


def kernel(
    tk_h, tg_h, ids_h, kw_h, gw_h, bias_h, gate_h, go_h, dw_h, bank_h, lids_h,
    out_ref,
    tk, tg, ids, kw, gw, bias, gate, go, dw, bank, lids,
    near, pbuf, rz, bbuf, br, hid, swt, uh_tx, uh_rx, uh_sum, uh_rs, ug_tx, ug_rx, ug_sum, ug_rs,
    uz_tx, uz, mm, ftx, frx,
    lsem, kwsem, rz_s, rz_r, b_s, b_r, i_s, i_r, a_s, a_r, c_s, c_r, x_s, x_r, z_s, z_r, f_s, f_r,
):
    d, m = lax.axis_index("dp"), lax.axis_index("mp")
    c = lax.rem(d, 2)
    q = lax.div(d, 2)
    y, x = lax.div(q, NX), lax.rem(q, NX)
    sibling = (d + 1 - 2 * c, m)

    def zdev(k):
        return (d, lax.rem(m + k, NZ))

    def chip(k):
        ky, kx = divmod(k, NX)
        return lax.rem(y + ky, NY) * NX + lax.rem(x + kx, NX)

    def rows_of(chip_index):
        return pl.ds(pl.multiple_of(lax.rem(chip_index + NCHIP // 2, NCHIP) * RB, RB), RB)

    def remote(src, dst, s, r, dev):
        pltpu.make_async_remote_copy(
            src_ref=src, dst_ref=dst, send_sem=s, recv_sem=r, device_id=dev, device_id_type=MESH
        ).start()

    waits = {}

    def expect(name, buf, sem):
        waits[name] = pltpu.make_async_copy(buf, buf, sem).wait

    def settle(name):
        waits.pop(name)()

    core_rows = pl.ds(pl.multiple_of(c * HALF, HALF), HALF)
    loads = dict(
        tk=(tk_h, tk), bank=(bank_h, bank), lids=(lids_h, lids), tg=(tg_h, tg), gw=(gw_h, gw),
        ids=(ids_h, ids), bias=(bias_h, bias), gate=(gate_h, gate),
        dw=(dw_h, dw), go=(go_h.at[core_rows], go),
    )
    number = {name: i for i, name in enumerate(loads)}

    def load(name):
        src, dst = loads[name]
        copy = pltpu.make_async_copy(src, dst, lsem.at[number[name]])
        copy.start()
        waits[name] = copy.wait

    def load_kw(ch):
        copy = pltpu.make_async_copy(kw_h.at[:, pl.ds(ch * CH, CH)], kw.at[ch], kwsem.at[ch])
        copy.start()
        waits["kw", ch] = copy.wait

    for name in ("tk", "bank", "lids", "ids", "tg", "gw"):
        load(name)
    for ch in range(NCH):
        load_kw(ch)
    for name in ("bias", "gate", "dw", "go"):
        load(name)

    barrier = pltpu.get_barrier_semaphore()
    beside = [lax.rem(d + 1, 2 * NCHIP), lax.rem(d + 2 * NCHIP - 1, 2 * NCHIP)]
    target = lax.rem(lax.div(d, 4) + NZ // 2, NZ)
    greet = [sibling] + [(e, m) for e in beside]
    greet += [zdev(k) for k in range(1, NZ)]
    greet += [(chip(k) * 2 + c, m) for k in range(1, NCHIP)]
    for dev in greet:
        pl.semaphore_signal(barrier, inc=1, device_id=dev, device_id_type=MESH)

    settle("lids")
    ids_row = lids[...].astype(F32)
    pick_t = (
        lax.broadcasted_iota(jnp.int32, (BANK, ROWS), 0).astype(F32) == ids_row
    ).astype(F32).astype(BF16)
    settle("tk")
    settle("bank")
    bank_scores = lax.dot_general(tk[...], bank[...], NT, preferred_element_type=F32).astype(BF16)
    pbuf[NCH] = jnp.dot(bank_scores, pick_t, preferred_element_type=F32).astype(BF16)

    def partial_sum(ch):
        if ch == 0:
            settle("tg")
            settle("gw")
        settle(("kw", ch))
        value = jnp.dot(tk[...], kw[ch], preferred_element_type=F32)
        value = value + jnp.dot(
            tg[...], gw[:, ch * CH:(ch + 1) * CH], preferred_element_type=F32
        )
        pbuf[ch] = value.astype(BF16)

    def send_partial(ch):
        for k in (4, 3, 5, 2, 6, 1, 7):
            to = lax.rem(m + k, NZ)
            rows = pl.ds(pl.multiple_of(to * TB, TB), TB)
            remote(pbuf.at[ch, rows], rz.at[ch, k - 1], rz_s.at[ch], rz_r.at[ch], (d, to))
        expect(("rz", ch), rz.at[ch], rz_r.at[ch])
        expect(("rz sent", ch), rz.at[ch], rz_s.at[ch])

    settle("ids")
    pl.semaphore_wait(barrier, len(greet))
    send_partial(NCH)
    partial_sum(0)
    send_partial(0)
    for i, e in enumerate(beside):
        remote(ids, near.at[i], i_s.at[i], i_r.at[i], (e, m))
        expect(("near", i), near.at[i], i_r.at[i])
        expect(("near sent", i), near.at[i], i_s.at[i])
    for ch in range(1, NCH):
        partial_sum(ch)
        send_partial(ch)

    own_ids = ids[...].astype(F32)
    wanted = lax.broadcasted_iota(jnp.int32, (TB, TOK), 1) == (
        lax.broadcasted_iota(jnp.int32, (TB, TOK), 0) + m * TB
    )
    ids_here = jnp.sum(jnp.where(wanted, jnp.broadcast_to(own_ids, (TB, TOK)), 0.0), axis=1, keepdims=True)
    count = jnp.sum((ids_here == own_ids).astype(F32), axis=1, keepdims=True)
    for i in range(2):
        settle(("near", i))
        count = count + jnp.sum((ids_here == near[i].astype(F32)).astype(F32), axis=1, keepdims=True)

    settle("bias")
    settle("gate")
    mine = pl.ds(pl.multiple_of(m * TB, TB), TB)

    def summed(ch):
        settle(("rz", ch))
        value = pbuf[ch, mine].astype(F32)
        for k in range(NZ - 1):
            value = value + rz[ch, k].astype(F32)
        return value

    gated = jnp.zeros((TB, 1), F32)
    for ch in range(NCH):
        cut = slice(ch * CH, (ch + 1) * CH)
        hidden = jnp.maximum(summed(ch) + bias[:, cut], 0.0).astype(BF16)
        hid[:, cut] = hidden
        gated = gated + jnp.sum(hidden.astype(F32) * gate[:, cut], axis=1, keepdims=True)
    weight = 2.0 / ((1.0 + jnp.exp(-gated)) * count)
    sw = (summed(NCH) * weight).astype(BF16)
    swt[mine] = sw

    def half(core):
        return pl.ds(pl.multiple_of(core * HALF, HALF), HALF)

    uh_tx[...] = lax.dot_general(sw, hid[:, half(1 - c)], TN, preferred_element_type=F32).astype(BF16)
    remote(uh_tx, uh_rx, c_s.at[0], c_r.at[0], sibling)
    expect("uh_rx", uh_rx, c_r.at[0])
    expect("uh_tx sent", uh_rx, c_s.at[0])
    for k in range(1, NZ):
        remote(swt.at[mine], swt.at[mine], a_s.at[0], a_r.at[0], zdev(k))
    expect("swt", swt.at[pl.ds(0, TOK - TB)], a_r.at[0])
    expect("swt sent", swt.at[pl.ds(0, TOK - TB)], a_s.at[0])
    own = lax.dot_general(sw, hid[:, half(c)], TN, preferred_element_type=F32)
    settle("uh_rx")
    uh_sum[...] = (own + uh_rx[...].astype(F32)).astype(BF16)
    for k in range(1, NCHIP):
        to = chip(k)
        remote(uh_sum.at[rows_of(to)], uh_rs.at[k - 1], x_s.at[0], x_r.at[0], (to * 2 + c, m))
    expect("uh_rs", uh_rs, x_r.at[0])
    expect("uh_rs sent", uh_rs, x_s.at[0])

    settle("dw")
    square = lax.broadcasted_iota(jnp.int32, (ROWS, ROWS), 0) == lax.broadcasted_iota(
        jnp.int32, (ROWS, ROWS), 1
    )
    ids_col = jnp.sum(jnp.where(square, jnp.broadcast_to(ids_row, (ROWS, ROWS)), 0.0), axis=1, keepdims=True)
    pick = (
        lax.broadcasted_iota(jnp.int32, (ROWS, BANK), 1).astype(F32) == ids_col
    ).astype(F32).astype(BF16)
    bank_down = lax.dot_general(bank[...], dw[...], NT, preferred_element_type=F32).astype(BF16)
    bbuf[...] = jnp.dot(pick, bank_down, preferred_element_type=F32).astype(BF16)
    for k in range(1, NZ):
        to = lax.rem(m + k, NZ)
        remote(
            bbuf.at[pl.ds(pl.multiple_of(to * OB, OB), OB)], br.at[k - 1], b_s.at[0], b_r.at[0], (d, to)
        )
    expect("br", br, b_r.at[0])
    expect("br sent", br, b_s.at[0])

    def window(core):
        return pl.ds(pl.multiple_of(core * 256, 256), WIDE)

    settle("swt")
    scores = swt[...]
    ug_tx[...] = lax.dot_general(scores, tg[:, window(1 - c)], TN, preferred_element_type=F32).astype(BF16)
    remote(ug_tx, ug_rx, c_s.at[1], c_r.at[1], sibling)
    expect("ug_rx", ug_rx, c_r.at[1])
    expect("ug_tx sent", ug_rx, c_s.at[1])
    own = lax.dot_general(scores, tg[:, window(c)], TN, preferred_element_type=F32)
    settle("ug_rx")
    ug_sum[...] = (own + ug_rx[...].astype(F32)).astype(BF16)
    for k in range(1, NCHIP):
        to = chip(k)
        remote(ug_sum.at[rows_of(to)], ug_rs.at[k - 1], x_s.at[1], x_r.at[1], (to * 2 + c, m))
    expect("ug_rs", ug_rs, x_r.at[1])
    expect("ug_rs sent", ug_rs, x_s.at[1])

    settle("uh_rs")
    value = uh_sum[rows_of(q)].astype(F32)
    for k in range(NCHIP - 1):
        value = value + uh_rs[k].astype(F32)
    uz_tx[...] = value.astype(BF16)
    for k in range(1, NZ):
        remote(uz_tx, uz.at[k - 1], z_s.at[0], z_r.at[0], zdev(k))
    expect("uz", uz, z_r.at[0])
    expect("uz sent", uz, z_s.at[0])

    settle("ug_rs")
    grads_part = ug_sum[rows_of(q)].astype(F32)
    for k in range(NCHIP - 1):
        grads_part = grads_part + ug_rs[k].astype(F32)
    lane = lax.broadcasted_iota(jnp.int32, (RB, WIDE), 1)
    grads_part = jnp.where(lane >= c * 128, grads_part, 0.0)

    settle("go")
    settle("uz")
    for k in range(NZ - 1):
        value = value + uz[k].astype(F32)
    mm[...] = jnp.dot(value.astype(BF16), go[...], preferred_element_type=F32)
    mm[:, window(c)] = mm[:, window(c)] + grads_part
    ftx[...] = mm[...].astype(BF16)
    slot = lax.rem(d, 4)
    for j in range(4):
        remote(ftx.at[:, pl.ds(128 * j, 256)], frx.at[slot], f_s.at[0], f_r.at[0], (4 * m + j, target))
    expect("frx", frx, f_r.at[0])
    expect("frx sent", frx, f_s.at[0])

    settle("br")
    base = bbuf[pl.ds(pl.multiple_of(m * OB, OB), OB)].astype(F32)
    for k in range(NZ - 1):
        base = base + br[k].astype(F32)
    settle("frx")
    spread = jnp.concatenate(
        [frx[0].astype(F32) + frx[1].astype(F32), frx[2].astype(F32) + frx[3].astype(F32)], axis=0
    )
    spread = pltpu.roll(spread, lax.rem(256 - 32 * slot, 256), 1)
    out_ref[...] = (base + SCALE * spread[:, :COLS]).astype(BF16)

    for name in list(waits):
        settle(name)


def local(
    token_keys, token_grads, prompt_ids, key_weight, grad_weight, hidden_bias, gate_vector, grad_output,
    down_weight, locality_bank, locality_ids,
):
    vm = pltpu.VMEM
    dma = pltpu.SemaphoreType.DMA
    scratch = [
        vm((TOK, KEYS), BF16), vm((TOK, GRADS), BF16), vm((1, TOK), jnp.int32),
        vm((NCH, KEYS, CH), BF16), vm((GRADS, HID), BF16), vm((1, HID), F32), vm((1, HID), F32),
        vm((HALF, GRADS), BF16), vm((COLS, KEYS), BF16), vm((BANK, KEYS), BF16), vm((1, ROWS), jnp.int32),
        vm((2, 1, TOK), jnp.int32),
        vm((NCH + 1, TOK, CH), BF16), vm((NCH + 1, NZ - 1, TB, CH), BF16),
        vm((ROWS, COLS), BF16), vm((NZ - 1, OB, COLS), BF16),
        vm((TB, HID), BF16), vm((TOK, ROWS), BF16),
        vm((ROWS, HALF), BF16), vm((ROWS, HALF), BF16), vm((ROWS, HALF), BF16),
        vm((NCHIP - 1, RB, HALF), BF16),
        vm((ROWS, WIDE), BF16), vm((ROWS, WIDE), BF16), vm((ROWS, WIDE), BF16),
        vm((NCHIP - 1, RB, WIDE), BF16),
        vm((RB, HALF), BF16), vm((NZ - 1, RB, HALF), BF16),
        vm((RB, GRADS), F32), vm((RB, GRADS), BF16), vm((4, RB, 256), BF16),
        dma((10,)), dma((NCH,)), dma((NCH + 1,)), dma((NCH + 1,)), dma((1,)), dma((1,)), dma((2,)), dma((2,)),
        dma((1,)), dma((1,)), dma((2,)), dma((2,)), dma((2,)), dma((2,)), dma((1,)), dma((1,)), dma((1,)), dma((1,)),
    ]
    any_spec = pl.BlockSpec(memory_space=pl.ANY)
    return pl.pallas_call(
        kernel,
        out_shape=pltpu.VMEM((OB, COLS), BF16),
        in_specs=[any_spec] * 11,
        out_specs=pl.BlockSpec(memory_space=pltpu.VMEM),
        scratch_shapes=scratch,
        compiler_params=pltpu.CompilerParams(
            collective_id=0, has_side_effects=True, vmem_limit_bytes=60 * 1024 * 1024
        ),
        cost_estimate=pl.CostEstimate(flops=2_000_000_000, bytes_accessed=14_000_000, transcendentals=16),
    )(
        token_keys, token_grads, prompt_ids.reshape(1, TOK), key_weight, grad_weight,
        hidden_bias.reshape(1, HID), gate_vector.reshape(1, HID), grad_output, down_weight.T, locality_bank,
        locality_ids.reshape(1, ROWS),
    )


def solution(mesh):
    placed = (
        P("dp", "mp"), P("dp", "mp"), P("dp"), P("mp", None), P("mp", None), P(), P(), P(None, "mp"),
        P("mp", "dp"), P(None, "mp"), P(),
    )
    return jax.shard_map(
        local, mesh=mesh, in_specs=placed, out_specs=P("mp", "dp"), check_vma=False
    )
```

```python
import jax
import jax.numpy as jnp
from jax import lax
from jax.experimental import pallas as pl
from jax.experimental.pallas import tpu as pltpu
from jax.sharding import PartitionSpec as P

MESH = pl.DeviceIdType.MESH
F32, BF16 = jnp.float32, jnp.bfloat16
NZ, NX, NY, NCHIP = 8, 4, 4, 16
TOK, KEYS, GRADS, HID, ROWS, BANK, COLS = 128, 3200, 640, 1024, 256, 320, 160
TB = TOK // NZ
RB = ROWS // NCHIP
HALF = HID // 2
WIDE = 384
CH = 256
NCH = HID // CH
OB = ROWS // NZ
SCALE = 4.0 / 10240.0

FAR = sorted(range(1, NCHIP), key=lambda k: -(min(k // NX, NY - k // NX) + min(k % NX, NX - k % NX)))

TN = (((0,), (0,)), ((), ()))
NT = (((1,), (1,)), ((), ()))


def kernel(
    tk_h, tg_h, ids_h, kw_h, gw_h, bias_h, gate_h, go_h, dw_h, bank_h, lids_h,
    out_ref,
    tk, tg, ids, kw, gw, bias, gate, go, dw, bank, lids,
    near, factor, pbuf, rz, bbuf, br, hid, sw2, hid2, swx, uh_sum, uh_rs, ug_sum, ug_rs,
    uz_tx, uz, ftx, frx, gtx, grx,
    lsem, kwsem, rz_s, rz_r, b_s, b_r, i_s, i_r, a_s, a_r, c_s, c_r, x_s, x_r, z_s, z_r, f_s, f_r, g_s, g_r,
):
    d, m = lax.axis_index("dp"), lax.axis_index("mp")
    c = lax.rem(d, 2)
    q = lax.div(d, 2)
    y, x = lax.div(q, NX), lax.rem(q, NX)
    sibling = (d + 1 - 2 * c, m)

    def zdev(k):
        return (d, lax.rem(m + k, NZ))

    def chip(k):
        ky, kx = divmod(k, NX)
        return lax.rem(y + ky, NY) * NX + lax.rem(x + kx, NX)

    def rows_of(chip_index):
        block = lax.rem(chip_index, 2) * NZ + lax.rem(lax.div(chip_index, 2) + NZ // 2, NZ)
        return pl.ds(pl.multiple_of(block * RB, RB), RB)

    def place(chip_index):
        dx = lax.rem(lax.rem(chip_index, NX) - 2 * lax.rem(m, 2) + NX, NX)
        dy = lax.rem(lax.div(chip_index, NX) - lax.div(m, 2) + NY, NY)
        side, far = lax.rem(lax.div(dx + 1, 2), 2), lax.div(dx, 2)
        step = (1 - far) * (lax.rem(dy + 2, 4) + 2) + far * lax.rem(dy + 6, 8)
        return side, lax.rem(m + step, NZ)

    def piece(chip_index):
        side, block = place(chip_index)
        return pl.ds(pl.multiple_of(block * RB, RB), RB), pl.ds(pl.multiple_of(side * 256, 256), WIDE)

    def remote(src, dst, s, r, dev):
        pltpu.make_async_remote_copy(
            src_ref=src, dst_ref=dst, send_sem=s, recv_sem=r, device_id=dev, device_id_type=MESH
        ).start()

    waits = {}

    def expect(name, buf, sem):
        waits[name] = pltpu.make_async_copy(buf, buf, sem).wait

    def settle(name):
        waits.pop(name)()

    core_tokens = pl.ds(pl.multiple_of(c * TOK, TOK), TOK)
    core_rows16 = pl.ds(pl.multiple_of(c * TB, TB), TB)
    core_rows = pl.ds(pl.multiple_of(c * HALF, HALF), HALF)
    loads = dict(
        tk=(tk_h, tk), bank=(bank_h, bank), lids=(lids_h, lids), tg=(tg_h, tg.at[core_tokens]),
        ids=(ids_h, ids), bias=(bias_h, bias), gate=(gate_h, gate),
        dw=(dw_h, dw), go=(go_h.at[core_rows], go),
    )
    number = {name: i for i, name in enumerate(loads)}

    def load(name):
        src, dst = loads[name]
        copy = pltpu.make_async_copy(src, dst, lsem.at[number[name]])
        copy.start()
        waits[name] = copy.wait

    def load_kw(ch):
        copy = pltpu.make_async_copy(kw_h.at[:, pl.ds(ch * CH, CH)], kw.at[ch], kwsem.at[ch])
        copy.start()
        waits["kw", ch] = copy.wait
        copy = pltpu.make_async_copy(gw_h.at[:, pl.ds(ch * CH, CH)], gw.at[ch], kwsem.at[NCH + ch])
        copy.start()
        waits["gw", ch] = copy.wait

    for name in ("lids", "tk", "bank", "tg", "ids", "bias", "gate"):
        load(name)

    barrier = pltpu.get_barrier_semaphore()
    beside = [lax.rem(d + 1, 2 * NCHIP), lax.rem(d + 2 * NCHIP - 1, 2 * NCHIP)]
    target = lax.rem(lax.div(d, 4) + NZ // 2, NZ)
    greet = [sibling] + [(e, m) for e in beside]
    greet += [zdev(k) for k in range(1, NZ)]
    greet += [(chip(k) * 2 + c, m) for k in range(1, NCHIP)]
    for dev in greet:
        pl.semaphore_signal(barrier, inc=1, device_id=dev, device_id_type=MESH)

    settle("lids")
    ids_row = lids[...].astype(F32)
    rows0 = lax.broadcasted_iota(jnp.int32, (ROWS, ROWS), 0)
    rows1 = lax.broadcasted_iota(jnp.int32, (ROWS, ROWS), 1)
    ids_col = jnp.sum(
        jnp.where(rows0 == rows1, jnp.broadcast_to(ids_row, (ROWS, ROWS)), 0.0), axis=1, keepdims=True
    )
    ordered = 32 * ((rows1 >> 4) & 7) + 16 * (rows1 >> 7) + (rows1 & 15)
    ids_ordered = jnp.sum(
        jnp.where(rows0 == ordered, jnp.broadcast_to(ids_col, (ROWS, ROWS)), 0.0), axis=0, keepdims=True
    )
    pick_t = (
        lax.broadcasted_iota(jnp.int32, (BANK, ROWS), 0).astype(F32) == ids_ordered
    ).astype(F32).astype(BF16)
    load_kw(0)
    settle("tk")
    settle("tg")

    def bank_part():
        settle("bank")
        bank_scores = lax.dot_general(tk[...], bank[...], NT, preferred_element_type=F32).astype(BF16)
        pbuf[NCH] = jnp.dot(bank_scores, pick_t, preferred_element_type=F32).astype(BF16)

    bank_part()
    load_kw(1)

    def partial_sum(ch):
        settle(("kw", ch))
        settle(("gw", ch))
        if ch + 2 < NCH:
            load_kw(ch + 2)
        elif ch + 2 == NCH:
            load("dw")
        else:
            load("go")
        value = jnp.dot(tk[...], kw[ch], preferred_element_type=F32)
        value = value + jnp.dot(
            tg[core_tokens], gw[ch], preferred_element_type=F32
        )
        pbuf[ch] = value.astype(BF16)

    def send_partial(first, many):
        for k in (4, 3, 5, 2, 6, 1, 7):
            to = lax.rem(m + k, NZ)
            rows = pl.ds(pl.multiple_of(to * TB, TB), TB)
            remote(
                pbuf.at[pl.ds(first, many), rows], rz.at[pl.ds(first, many), k - 1],
                rz_s.at[first], rz_r.at[first], (d, to),
            )
        expect(("rz", first), rz.at[pl.ds(first, many)], rz_r.at[first])
        expect(("rz sent", first), rz.at[pl.ds(first, many)], rz_s.at[first])

    settle("ids")
    pl.semaphore_wait(barrier, len(greet))
    send_partial(NCH, 1)
    partial_sum(0)
    send_partial(0, 1)
    remote(tg.at[core_tokens], tg.at[core_tokens], c_s.at[2], c_r.at[2], sibling)
    expect("tg other", tg.at[core_tokens], c_r.at[2])
    expect("tg sent", tg.at[core_tokens], c_s.at[2])
    for i, e in enumerate(beside):
        remote(ids, near.at[i], i_s.at[i], i_r.at[i], (e, m))
        expect(("near", i), near.at[i], i_r.at[i])
        expect(("near sent", i), near.at[i], i_s.at[i])
    for ch in range(1, NCH):
        partial_sum(ch)
        if ch == NCH - 1:
            send_partial(1, 3)

    own_ids = ids[...].astype(F32)
    wanted = lax.broadcasted_iota(jnp.int32, (TB, TOK), 1) == (
        lax.broadcasted_iota(jnp.int32, (TB, TOK), 0) + m * TB
    )
    ids_here = jnp.sum(jnp.where(wanted, jnp.broadcast_to(own_ids, (TB, TOK)), 0.0), axis=1, keepdims=True)
    count = jnp.sum((ids_here == own_ids).astype(F32), axis=1, keepdims=True)
    for i in range(2):
        settle(("near", i))
        count = count + jnp.sum((ids_here == near[i].astype(F32)).astype(F32), axis=1, keepdims=True)

    factor[...] = jnp.broadcast_to(2.0 / count, (TB, ROWS))
    settle("bias")
    settle("gate")
    mine = pl.ds(pl.multiple_of(m * TB, TB), TB)

    def summed(ch):
        if ("rz", ch) in waits:
            settle(("rz", ch))
        value = pbuf[ch, mine].astype(F32)
        for k in range(NZ - 1):
            value = value + rz[ch, k].astype(F32)
        return value

    gated = jnp.zeros((TB, CH), F32)
    for ch in range(NCH):
        cut = slice(ch * CH, (ch + 1) * CH)
        hidden = jnp.maximum(summed(ch) + bias[:, cut], 0.0).astype(BF16)
        hid[:, cut] = hidden
        gated = gated + hidden.astype(F32) * gate[:, cut]
    weight = jax.nn.sigmoid(jnp.sum(gated, axis=1, keepdims=True)) * factor[...]
    def half(core):
        return pl.ds(pl.multiple_of(core * HALF, HALF), HALF)

    remote(hid.at[:, half(1 - c)], hid2.at[core_rows16], c_s.at[1], c_r.at[1], sibling)
    expect("hid2", hid2.at[core_rows16], c_r.at[1])
    expect("hid2 sent", hid2.at[core_rows16], c_s.at[1])
    hid2[core_rows16] = hid[:, half(c)]
    sw2[core_rows16] = (summed(NCH) * weight).astype(BF16)
    remote(sw2.at[core_rows16], sw2.at[core_rows16], c_s.at[0], c_r.at[0], sibling)
    expect("sw2", sw2.at[core_rows16], c_r.at[0])
    expect("sw2 sent", sw2.at[core_rows16], c_s.at[0])

    def lanes(core):
        return pl.ds(pl.multiple_of(core * 128, 128), 128)

    my_tokens = pl.ds(pl.multiple_of(c * TOK + m * TB, TB), TB)

    def send_scores(core, k):
        remote(
            sw2.at[core_rows16, lanes(core)], swx.at[my_tokens], a_s.at[0], a_r.at[0],
            (q * 2 + core, lax.rem(m + k, NZ)),
        )

    settle("hid2")
    settle("sw2")
    for part in range(2):
        units = slice(part * CH, (part + 1) * CH)
        uh_sum[part] = lax.dot_general(sw2[...], hid2[:, units], TN, preferred_element_type=F32).astype(BF16)
        for k in FAR:
            to = chip(k)
            remote(
                uh_sum.at[part, rows_of(to)], uh_rs.at[part, k - 1], x_s.at[part], x_r.at[part], (to * 2 + c, m)
            )
        expect(("uh_rs", part), uh_rs.at[part], x_r.at[part])
        expect(("uh_rs sent", part), uh_rs.at[part], x_s.at[part])

    swx[my_tokens] = sw2[core_rows16, lanes(c)]
    for k in (4, 3, 5, 2, 6, 1, 7):
        for core in range(2):
            send_scores(core, k)
    send_scores(1 - c, 0)
    expect("swx", swx.at[pl.ds(0, 2 * TOK - TB)], a_r.at[0])
    expect("swx sent", swx.at[pl.ds(0, 2 * TOK - TB)], a_s.at[0])

    settle("dw")
    pick = (
        lax.broadcasted_iota(jnp.int32, (ROWS, BANK), 1).astype(F32) == ids_col
    ).astype(F32).astype(BF16)
    bank_down = lax.dot_general(bank[...], dw[...], NT, preferred_element_type=F32).astype(BF16)
    bbuf[...] = jnp.dot(pick, bank_down, preferred_element_type=F32).astype(BF16)
    for k in range(1, NZ):
        to = lax.rem(m + k, NZ)
        remote(
            bbuf.at[pl.ds(pl.multiple_of(to * OB, OB), OB)], br.at[k - 1], b_s.at[0], b_r.at[0], (d, to)
        )
    expect("br", br, b_r.at[0])
    expect("br sent", br, b_s.at[0])

    settle("tg other")
    settle("swx")
    ug_sum[...] = lax.dot_general(swx[...], tg[...], TN, preferred_element_type=F32).astype(BF16)
    for k in FAR:
        to = chip(k)
        remote(ug_sum.at[piece(to)], ug_rs.at[k - 1], x_s.at[2], x_r.at[2], (to * 2 + c, m))
    expect("ug_rs", ug_rs, x_r.at[2])
    expect("ug_rs sent", ug_rs, x_s.at[2])

    plane = []
    for part in range(2):
        settle(("uh_rs", part))
        value = uh_sum[part, rows_of(q)].astype(F32)
        for k in range(NCHIP - 1):
            value = value + uh_rs[part, k].astype(F32)
        plane.append(value)
        uz_tx[part] = value.astype(BF16)
        for k in (4, 3, 5, 2, 6, 1, 7):
            remote(uz_tx.at[part], uz.at[part, k - 1], z_s.at[part], z_r.at[part], zdev(k))
        expect(("uz", part), uz.at[part], z_r.at[part])
        expect(("uz sent", part), uz.at[part], z_s.at[part])

    settle("ug_rs")
    grads_part = ug_sum[piece(q)].astype(F32)
    for k in range(NCHIP - 1):
        grads_part = grads_part + ug_rs[k].astype(F32)
    gtx[...] = grads_part.astype(BF16)
    side, block = place(q)
    for j in range(2):
        remote(
            gtx.at[:, pl.ds(128 * j, 256)], grx.at[c], g_s.at[0], g_r.at[0], (4 * m + 2 * side + j, block)
        )
    expect("grx", grx, g_r.at[0])
    expect("grx sent", grx, g_s.at[0])

    settle("go")
    product = jnp.zeros((RB, GRADS), F32)
    for part in range(2):
        settle(("uz", part))
        value = plane[part]
        for k in range(NZ - 1):
            value = value + uz[part, k].astype(F32)
        product = product + jnp.dot(
            value.astype(BF16), go[part * CH:(part + 1) * CH], preferred_element_type=F32
        )
    ftx[...] = product.astype(BF16)
    slot = lax.rem(d, 4)
    for j in range(4):
        remote(ftx.at[:, pl.ds(128 * j, 256)], frx.at[slot], f_s.at[0], f_r.at[0], (4 * m + j, target))
    expect("frx", frx, f_r.at[0])
    expect("frx sent", frx, f_s.at[0])

    settle("br")
    base = bbuf[pl.ds(pl.multiple_of(m * OB, OB), OB)].astype(F32)
    for k in range(NZ - 1):
        base = base + br[k].astype(F32)
    settle("grx")
    settle("frx")
    spread = jnp.concatenate(
        [
            frx[0].astype(F32) + frx[1].astype(F32) + grx[0].astype(F32),
            frx[2].astype(F32) + frx[3].astype(F32) + grx[1].astype(F32),
        ],
        axis=0,
    )
    spread = pltpu.roll(spread, lax.rem(256 - 32 * slot, 256), 1)
    out_ref[...] = (base + SCALE * spread[:, :COLS]).astype(BF16)

    for name in list(waits):
        settle(name)


def local(
    token_keys, token_grads, prompt_ids, key_weight, grad_weight, hidden_bias, gate_vector, grad_output,
    down_weight, locality_bank, locality_ids,
):
    vm = pltpu.VMEM
    dma = pltpu.SemaphoreType.DMA
    scratch = [
        vm((TOK, KEYS), BF16), vm((2 * TOK, GRADS), BF16), vm((1, TOK), jnp.int32),
        vm((NCH, KEYS, CH), BF16), vm((NCH, GRADS, CH), BF16), vm((1, HID), F32), vm((1, HID), F32),
        vm((HALF, GRADS), BF16), vm((COLS, KEYS), BF16), vm((BANK, KEYS), BF16), vm((1, ROWS), jnp.int32),
        vm((2, 1, TOK), jnp.int32), vm((TB, ROWS), F32),
        vm((NCH + 1, TOK, CH), BF16), vm((NCH + 1, NZ - 1, TB, CH), BF16),
        vm((ROWS, COLS), BF16), vm((NZ - 1, OB, COLS), BF16),
        vm((TB, HID), BF16), vm((2 * TB, ROWS), BF16), vm((2 * TB, HALF), BF16), vm((2 * TOK, 128), BF16),
        vm((2, ROWS, CH), BF16), vm((2, NCHIP - 1, RB, CH), BF16),
        vm((ROWS // 2, GRADS), BF16), vm((NCHIP - 1, RB, WIDE), BF16),
        vm((2, RB, CH), BF16), vm((2, NZ - 1, RB, CH), BF16),
        vm((RB, GRADS), BF16), vm((4, RB, 256), BF16), vm((RB, WIDE), BF16), vm((2, RB, 256), BF16),
        dma((10,)), dma((2 * NCH,)), dma((NCH + 1,)), dma((NCH + 1,)), dma((1,)), dma((1,)), dma((2,)), dma((2,)),
        dma((1,)), dma((1,)), dma((3,)), dma((3,)), dma((3,)), dma((3,)), dma((2,)), dma((2,)), dma((1,)), dma((1,)),
        dma((1,)), dma((1,)),
    ]
    any_spec = pl.BlockSpec(memory_space=pl.ANY)
    return pl.pallas_call(
        kernel,
        out_shape=pltpu.VMEM((OB, COLS), BF16),
        in_specs=[any_spec] * 11,
        out_specs=pl.BlockSpec(memory_space=pltpu.VMEM),
        scratch_shapes=scratch,
        compiler_params=pltpu.CompilerParams(
            collective_id=0, has_side_effects=True, vmem_limit_bytes=60 * 1024 * 1024
        ),
        cost_estimate=pl.CostEstimate(flops=2_000_000_000, bytes_accessed=14_000_000, transcendentals=16),
    )(
        token_keys, token_grads, prompt_ids.reshape(1, TOK), key_weight, grad_weight,
        hidden_bias.reshape(1, HID), gate_vector.reshape(1, HID), grad_output, down_weight.T, locality_bank,
        locality_ids.reshape(1, ROWS),
    )


def solution(mesh):
    placed = (
        P("dp", "mp"), P("dp", "mp"), P("dp"), P("mp", None), P("mp", None), P(), P(), P(None, "mp"),
        P("mp", "dp"), P(None, "mp"), P(),
    )
    return jax.shard_map(
        local, mesh=mesh, in_specs=placed, out_specs=P("mp", "dp"), check_vma=False
    )
```

```python
import jax
import jax.numpy as jnp
from jax import lax
from jax.experimental import pallas as pl
from jax.experimental.pallas import tpu as pltpu
from jax.sharding import PartitionSpec as P

MESH = pl.DeviceIdType.MESH
F32, BF16 = jnp.float32, jnp.bfloat16
NZ, NX, NY, NCHIP = 8, 4, 4, 16
TOK, KEYS, GRADS, HID, ROWS, BANK, COLS = 128, 3200, 640, 1024, 256, 320, 160
TB = TOK // NZ
RB = ROWS // NCHIP
HALF = HID // 2
WIDE = 384
CH = 256
NCH = HID // CH
OB = ROWS // NZ
SCALE = 4.0 / 10240.0

FAR = sorted(range(1, NCHIP), key=lambda k: -(min(k // NX, NY - k // NX) + min(k % NX, NX - k % NX)))

TN = (((0,), (0,)), ((), ()))
NT = (((1,), (1,)), ((), ()))


def kernel(
    tk_h, tg_h, ids_h, kw_h, gw_h, bias_h, gate_h, go_h, dw_h, bank_h, lids_h,
    out_ref,
    tk, tg, ids, kw, gw, bias, gate, go, dw, bank, lids,
    near, factor, pbuf, rz, bbuf, br, hid, sw2, hid2, swx, uh_sum, uh_rs, ug_sum, ug_rs,
    uz_tx, uz, ftx, frx, gtx, grx,
    lsem, kwsem, rz_s, rz_r, b_s, b_r, i_s, i_r, a_s, a_r, c_s, c_r, x_s, x_r, z_s, z_r, f_s, f_r, g_s, g_r,
):
    d, m = lax.axis_index("dp"), lax.axis_index("mp")
    c = lax.rem(d, 2)
    q = lax.div(d, 2)
    y, x = lax.div(q, NX), lax.rem(q, NX)
    sibling = (d + 1 - 2 * c, m)

    def zdev(k):
        return (d, lax.rem(m + k, NZ))

    def chip(k):
        ky, kx = divmod(k, NX)
        return lax.rem(y + ky, NY) * NX + lax.rem(x + kx, NX)

    def rows_of(chip_index):
        block = lax.rem(chip_index, 2) * NZ + lax.rem(lax.div(chip_index, 2) + NZ // 2, NZ)
        return pl.ds(pl.multiple_of(block * RB, RB), RB)

    def place(chip_index):
        dx = lax.rem(lax.rem(chip_index, NX) - 2 * lax.rem(m, 2) + NX, NX)
        dy = lax.rem(lax.div(chip_index, NX) - lax.div(m, 2) + NY, NY)
        side, far = lax.rem(lax.div(dx + 1, 2), 2), lax.div(dx, 2)
        step = (1 - far) * (lax.rem(dy + 2, 4) + 2) + far * lax.rem(dy + 6, 8)
        return side, lax.rem(m + step, NZ)

    def piece(chip_index):
        side, block = place(chip_index)
        return pl.ds(pl.multiple_of(block * RB, RB), RB), pl.ds(pl.multiple_of(side * 256, 256), WIDE)

    def remote(src, dst, s, r, dev):
        pltpu.make_async_remote_copy(
            src_ref=src, dst_ref=dst, send_sem=s, recv_sem=r, device_id=dev, device_id_type=MESH
        ).start()

    barrier = pltpu.get_barrier_semaphore()
    beside = [lax.rem(d + 1, 2 * NCHIP), lax.rem(d + 2 * NCHIP - 1, 2 * NCHIP)]
    target = lax.rem(lax.div(d, 4) + NZ // 2, NZ)
    greet = [zdev(k) for k in (4, 3, 5, 2, 6, 1, 7)]
    greet += [(chip(k) * 2 + c, m) for k in FAR]
    greet += [sibling] + [(e, m) for e in beside]
    for dev in greet:
        pl.semaphore_signal(barrier, inc=1, device_id=dev, device_id_type=MESH)

    waits = {}

    def expect(name, buf, sem):
        waits[name] = pltpu.make_async_copy(buf, buf, sem).wait

    def settle(name):
        waits.pop(name)()

    core_tokens = pl.ds(pl.multiple_of(c * TOK, TOK), TOK)
    core_rows16 = pl.ds(pl.multiple_of(c * TB, TB), TB)
    core_rows = pl.ds(pl.multiple_of(c * HALF, HALF), HALF)
    loads = dict(
        tk=(tk_h, tk), bank=(bank_h, bank), lids=(lids_h, lids), tg=(tg_h, tg.at[core_tokens]),
        ids=(ids_h, ids), bias=(bias_h, bias), gate=(gate_h, gate),
        dw=(dw_h, dw), go=(go_h.at[core_rows], go),
    )
    number = {name: i for i, name in enumerate(loads)}

    def load(name):
        src, dst = loads[name]
        copy = pltpu.make_async_copy(src, dst, lsem.at[number[name]])
        copy.start()
        waits[name] = copy.wait

    def load_kw(ch):
        copy = pltpu.make_async_copy(kw_h.at[:, pl.ds(ch * CH, CH)], kw.at[ch], kwsem.at[ch])
        copy.start()
        waits["kw", ch] = copy.wait
        copy = pltpu.make_async_copy(gw_h.at[:, pl.ds(ch * CH, CH)], gw.at[ch], kwsem.at[NCH + ch])
        copy.start()
        waits["gw", ch] = copy.wait

    for name in ("lids", "tk", "bank", "tg", "ids", "bias", "gate"):
        load(name)

    settle("lids")
    ids_row = lids[...].astype(F32)
    rows0 = lax.broadcasted_iota(jnp.int32, (ROWS, ROWS), 0)
    rows1 = lax.broadcasted_iota(jnp.int32, (ROWS, ROWS), 1)
    ids_col = jnp.sum(
        jnp.where(rows0 == rows1, jnp.broadcast_to(ids_row, (ROWS, ROWS)), 0.0), axis=1, keepdims=True
    )
    ordered = 32 * ((rows1 >> 4) & 7) + 16 * (rows1 >> 7) + (rows1 & 15)
    ids_ordered = jnp.sum(
        jnp.where(rows0 == ordered, jnp.broadcast_to(ids_col, (ROWS, ROWS)), 0.0), axis=0, keepdims=True
    )
    pick_t = (
        lax.broadcasted_iota(jnp.int32, (BANK, ROWS), 0).astype(F32) == ids_ordered
    ).astype(F32).astype(BF16)
    load_kw(0)
    settle("tk")
    settle("tg")

    def bank_part():
        settle("bank")
        bank_scores = lax.dot_general(tk[...], bank[...], NT, preferred_element_type=F32).astype(BF16)
        pbuf[NCH] = jnp.dot(bank_scores, pick_t, preferred_element_type=F32).astype(BF16)

    bank_part()
    load_kw(1)

    def partial_sum(ch):
        settle(("kw", ch))
        settle(("gw", ch))
        if ch + 2 < NCH:
            load_kw(ch + 2)
        elif ch + 2 == NCH:
            load("dw")
        else:
            load("go")
        value = jnp.dot(tk[...], kw[ch], preferred_element_type=F32)
        value = value + jnp.dot(
            tg[core_tokens], gw[ch], preferred_element_type=F32
        )
        pbuf[ch] = value.astype(BF16)

    def send_partial(first, many):
        for k in (4, 3, 5, 2, 6, 1, 7):
            to = lax.rem(m + k, NZ)
            rows = pl.ds(pl.multiple_of(to * TB, TB), TB)
            remote(
                pbuf.at[pl.ds(first, many), rows], rz.at[pl.ds(first, many), k - 1],
                rz_s.at[first], rz_r.at[first], (d, to),
            )
        expect(("rz", first), rz.at[pl.ds(first, many)], rz_r.at[first])
        expect(("rz sent", first), rz.at[pl.ds(first, many)], rz_s.at[first])

    settle("ids")
    pl.semaphore_wait(barrier, len(greet))
    send_partial(NCH, 1)
    partial_sum(0)
    send_partial(0, 1)
    remote(tg.at[core_tokens], tg.at[core_tokens], c_s.at[2], c_r.at[2], sibling)
    expect("tg other", tg.at[core_tokens], c_r.at[2])
    expect("tg sent", tg.at[core_tokens], c_s.at[2])
    for i, e in enumerate(beside):
        remote(ids, near.at[i], i_s.at[i], i_r.at[i], (e, m))
        expect(("near", i), near.at[i], i_r.at[i])
        expect(("near sent", i), near.at[i], i_s.at[i])
    for ch in range(1, NCH):
        partial_sum(ch)
        if ch == NCH - 1:
            send_partial(1, 3)

    settle("dw")
    pick = (
        lax.broadcasted_iota(jnp.int32, (ROWS, BANK), 1).astype(F32) == ids_col
    ).astype(F32).astype(BF16)
    bank_down = lax.dot_general(bank[...], dw[...], NT, preferred_element_type=F32).astype(BF16)
    bbuf[...] = jnp.dot(pick, bank_down, preferred_element_type=F32).astype(BF16)

    own_ids = ids[...].astype(F32)
    wanted = lax.broadcasted_iota(jnp.int32, (TB, TOK), 1) == (
        lax.broadcasted_iota(jnp.int32, (TB, TOK), 0) + m * TB
    )
    ids_here = jnp.sum(jnp.where(wanted, jnp.broadcast_to(own_ids, (TB, TOK)), 0.0), axis=1, keepdims=True)
    count = jnp.sum((ids_here == own_ids).astype(F32), axis=1, keepdims=True)
    for i in range(2):
        settle(("near", i))
        count = count + jnp.sum((ids_here == near[i].astype(F32)).astype(F32), axis=1, keepdims=True)

    factor[...] = jnp.broadcast_to(2.0 / count, (TB, ROWS))
    settle("bias")
    settle("gate")
    mine = pl.ds(pl.multiple_of(m * TB, TB), TB)

    def summed(ch):
        if ("rz", ch) in waits:
            settle(("rz", ch))
        value = pbuf[ch, mine].astype(F32)
        for k in range(NZ - 1):
            value = value + rz[ch, k].astype(F32)
        return value

    gated = jnp.zeros((TB, CH), F32)
    for ch in range(NCH):
        cut = slice(ch * CH, (ch + 1) * CH)
        hidden = jnp.maximum(summed(ch) + bias[:, cut], 0.0).astype(BF16)
        hid[:, cut] = hidden
        gated = gated + hidden.astype(F32) * gate[:, cut]
    weight = jax.nn.sigmoid(jnp.sum(gated, axis=1, keepdims=True)) * factor[...]
    def half(core):
        return pl.ds(pl.multiple_of(core * HALF, HALF), HALF)

    remote(hid.at[:, half(1 - c)], hid2.at[core_rows16], c_s.at[1], c_r.at[1], sibling)
    expect("hid2", hid2.at[core_rows16], c_r.at[1])
    expect("hid2 sent", hid2.at[core_rows16], c_s.at[1])
    hid2[core_rows16] = hid[:, half(c)]
    sw2[core_rows16] = (summed(NCH) * weight).astype(BF16)
    remote(sw2.at[core_rows16], sw2.at[core_rows16], c_s.at[0], c_r.at[0], sibling)
    expect("sw2", sw2.at[core_rows16], c_r.at[0])
    expect("sw2 sent", sw2.at[core_rows16], c_s.at[0])

    def lanes(core):
        return pl.ds(pl.multiple_of(core * 128, 128), 128)

    my_tokens = pl.ds(pl.multiple_of(c * TOK + m * TB, TB), TB)

    def send_scores(core, k):
        remote(
            sw2.at[core_rows16, lanes(core)], swx.at[my_tokens], a_s.at[0], a_r.at[0],
            (q * 2 + core, lax.rem(m + k, NZ)),
        )

    swx[my_tokens] = sw2[core_rows16, lanes(c)]
    for k in (4, 3, 5, 2, 6, 1, 7):
        for core in range(2):
            send_scores(core, k)
    send_scores(1 - c, 0)
    expect("swx", swx.at[pl.ds(0, 2 * TOK - TB)], a_r.at[0])
    expect("swx sent", swx.at[pl.ds(0, 2 * TOK - TB)], a_s.at[0])

    settle("hid2")
    settle("sw2")
    for part in range(2):
        units = slice(part * CH, (part + 1) * CH)
        uh_sum[part] = lax.dot_general(sw2[...], hid2[:, units], TN, preferred_element_type=F32).astype(BF16)
        for k in FAR:
            to = chip(k)
            remote(
                uh_sum.at[part, rows_of(to)], uh_rs.at[part, k - 1], x_s.at[part], x_r.at[part], (to * 2 + c, m)
            )
        expect(("uh_rs", part), uh_rs.at[part], x_r.at[part])
        expect(("uh_rs sent", part), uh_rs.at[part], x_s.at[part])

    for k in range(1, NZ):
        to = lax.rem(m + k, NZ)
        remote(
            bbuf.at[pl.ds(pl.multiple_of(to * OB, OB), OB)], br.at[k - 1], b_s.at[0], b_r.at[0], (d, to)
        )
    expect("br", br, b_r.at[0])
    expect("br sent", br, b_s.at[0])

    settle("tg other")
    settle("swx")
    ug_sum[...] = lax.dot_general(swx[...], tg[...], TN, preferred_element_type=F32).astype(BF16)
    for k in FAR:
        to = chip(k)
        remote(ug_sum.at[piece(to)], ug_rs.at[k - 1], x_s.at[2], x_r.at[2], (to * 2 + c, m))
    expect("ug_rs", ug_rs, x_r.at[2])
    expect("ug_rs sent", ug_rs, x_s.at[2])

    plane = []
    for part in range(2):
        settle(("uh_rs", part))
        value = uh_sum[part, rows_of(q)].astype(F32)
        for k in range(NCHIP - 1):
            value = value + uh_rs[part, k].astype(F32)
        plane.append(value)
        uz_tx[part] = value.astype(BF16)
        for k in (4, 3, 5, 2, 6, 1, 7):
            remote(uz_tx.at[part], uz.at[part, k - 1], z_s.at[part], z_r.at[part], zdev(k))
        expect(("uz", part), uz.at[part], z_r.at[part])
        expect(("uz sent", part), uz.at[part], z_s.at[part])

    settle("go")
    product = jnp.zeros((RB, GRADS), F32)
    for part in range(2):
        settle(("uz", part))
        value = plane[part]
        for k in range(NZ - 1):
            value = value + uz[part, k].astype(F32)
        product = product + jnp.dot(
            value.astype(BF16), go[part * CH:(part + 1) * CH], preferred_element_type=F32
        )
    ftx[...] = product.astype(BF16)
    slot = lax.rem(d, 4)
    for j in range(4):
        remote(ftx.at[:, pl.ds(128 * j, 256)], frx.at[slot], f_s.at[0], f_r.at[0], (4 * m + j, target))
    expect("frx", frx, f_r.at[0])
    expect("frx sent", frx, f_s.at[0])

    settle("ug_rs")
    grads_part = ug_sum[piece(q)].astype(F32)
    for k in range(NCHIP - 1):
        grads_part = grads_part + ug_rs[k].astype(F32)
    gtx[...] = grads_part.astype(BF16)
    side, block = place(q)
    for j in range(2):
        remote(
            gtx.at[:, pl.ds(128 * j, 256)], grx.at[c], g_s.at[0], g_r.at[0], (4 * m + 2 * side + j, block)
        )
    expect("grx", grx, g_r.at[0])
    expect("grx sent", grx, g_s.at[0])

    settle("br")
    base = bbuf[pl.ds(pl.multiple_of(m * OB, OB), OB)].astype(F32)
    for k in range(NZ - 1):
        base = base + br[k].astype(F32)
    settle("grx")
    settle("frx")
    spread = jnp.concatenate(
        [
            frx[0].astype(F32) + frx[1].astype(F32) + grx[0].astype(F32),
            frx[2].astype(F32) + frx[3].astype(F32) + grx[1].astype(F32),
        ],
        axis=0,
    )
    spread = pltpu.roll(spread, lax.rem(256 - 32 * slot, 256), 1)
    out_ref[...] = (base + SCALE * spread[:, :COLS]).astype(BF16)

    for name in list(waits):
        settle(name)


def local(
    token_keys, token_grads, prompt_ids, key_weight, grad_weight, hidden_bias, gate_vector, grad_output,
    down_weight, locality_bank, locality_ids,
):
    vm = pltpu.VMEM
    dma = pltpu.SemaphoreType.DMA
    scratch = [
        vm((TOK, KEYS), BF16), vm((2 * TOK, GRADS), BF16), vm((1, TOK), jnp.int32),
        vm((NCH, KEYS, CH), BF16), vm((NCH, GRADS, CH), BF16), vm((1, HID), F32), vm((1, HID), F32),
        vm((HALF, GRADS), BF16), vm((COLS, KEYS), BF16), vm((BANK, KEYS), BF16), vm((1, ROWS), jnp.int32),
        vm((2, 1, TOK), jnp.int32), vm((TB, ROWS), F32),
        vm((NCH + 1, TOK, CH), BF16), vm((NCH + 1, NZ - 1, TB, CH), BF16),
        vm((ROWS, COLS), BF16), vm((NZ - 1, OB, COLS), BF16),
        vm((TB, HID), BF16), vm((2 * TB, ROWS), BF16), vm((2 * TB, HALF), BF16), vm((2 * TOK, 128), BF16),
        vm((2, ROWS, CH), BF16), vm((2, NCHIP - 1, RB, CH), BF16),
        vm((ROWS // 2, GRADS), BF16), vm((NCHIP - 1, RB, WIDE), BF16),
        vm((2, RB, CH), BF16), vm((2, NZ - 1, RB, CH), BF16),
        vm((RB, GRADS), BF16), vm((4, RB, 256), BF16), vm((RB, WIDE), BF16), vm((2, RB, 256), BF16),
        dma((10,)), dma((2 * NCH,)), dma((NCH + 1,)), dma((NCH + 1,)), dma((1,)), dma((1,)), dma((2,)), dma((2,)),
        dma((1,)), dma((1,)), dma((3,)), dma((3,)), dma((3,)), dma((3,)), dma((2,)), dma((2,)), dma((1,)), dma((1,)),
        dma((1,)), dma((1,)),
    ]
    any_spec = pl.BlockSpec(memory_space=pl.ANY)
    return pl.pallas_call(
        kernel,
        out_shape=pltpu.VMEM((OB, COLS), BF16),
        in_specs=[any_spec] * 11,
        out_specs=pl.BlockSpec(memory_space=pltpu.VMEM),
        scratch_shapes=scratch,
        compiler_params=pltpu.CompilerParams(
            collective_id=0, has_side_effects=True, vmem_limit_bytes=60 * 1024 * 1024
        ),
        cost_estimate=pl.CostEstimate(flops=2_000_000_000, bytes_accessed=14_000_000, transcendentals=16),
    )(
        token_keys, token_grads, prompt_ids.reshape(1, TOK), key_weight, grad_weight,
        hidden_bias.reshape(1, HID), gate_vector.reshape(1, HID), grad_output, down_weight.T, locality_bank,
        locality_ids.reshape(1, ROWS),
    )


def solution(mesh):
    placed = (
        P("dp", "mp"), P("dp", "mp"), P("dp"), P("mp", None), P("mp", None), P(), P(), P(None, "mp"),
        P("mp", "dp"), P(None, "mp"), P(),
    )
    return jax.shard_map(
        local, mesh=mesh, in_specs=placed, out_specs=P("mp", "dp"), check_vma=False
    )
```

```python
import jax
import jax.numpy as jnp
from jax import lax
from jax.experimental import pallas as pl
from jax.experimental.pallas import tpu as pltpu
from jax.sharding import PartitionSpec as P

MESH = pl.DeviceIdType.MESH
F32, BF16 = jnp.float32, jnp.bfloat16
NZ, NX, NY, NCHIP = 8, 4, 4, 16
TOK, KEYS, GRADS, HID, ROWS, BANK, COLS = 128, 3200, 640, 1024, 256, 320, 160
TB = TOK // NZ
RB = ROWS // NCHIP
HALF = HID // 2
WIDE = 384
CH = 256
NCH = HID // CH
OB = ROWS // NZ
SCALE = 4.0 / 10240.0

FAR = sorted(range(1, NCHIP), key=lambda k: -(min(k // NX, NY - k // NX) + min(k % NX, NX - k % NX)))

TN = (((0,), (0,)), ((), ()))
NT = (((1,), (1,)), ((), ()))


def kernel(
    tk_h, tg_h, ids_h, kw_h, gw_h, bias_h, gate_h, go_h, dw_h, bank_h, lids_h,
    out_ref,
    tk, tg, ids, kw, gw, bias, gate, go, dw, bank, lids,
    near, factor, pbuf, rz, bbuf, br, hid, sw2, hid2, swx, uh_sum, uh_rs, ug_sum, ug_rs,
    uz_tx, uz, ftx, frx, gtx, grx,
    lsem, kwsem, rz_s, rz_r, b_s, b_r, i_s, i_r, a_s, a_r, c_s, c_r, x_s, x_r, z_s, z_r, f_s, f_r, g_s, g_r,
):
    d, m = lax.axis_index("dp"), lax.axis_index("mp")
    c = lax.rem(d, 2)
    q = lax.div(d, 2)
    y, x = lax.div(q, NX), lax.rem(q, NX)
    sibling = (d + 1 - 2 * c, m)

    def zdev(k):
        return (d, lax.rem(m + k, NZ))

    def chip(k):
        ky, kx = divmod(k, NX)
        return lax.rem(y + ky, NY) * NX + lax.rem(x + kx, NX)

    def rows_of(chip_index):
        block = lax.rem(chip_index, 2) * NZ + lax.rem(lax.div(chip_index, 2) + NZ // 2, NZ)
        return pl.ds(pl.multiple_of(block * RB, RB), RB)

    def place(chip_index):
        dx = lax.rem(lax.rem(chip_index, NX) - 2 * lax.rem(m, 2) + NX, NX)
        dy = lax.rem(lax.div(chip_index, NX) - lax.div(m, 2) + NY, NY)
        side, far = lax.rem(lax.div(dx + 1, 2), 2), lax.div(dx, 2)
        step = (1 - far) * (lax.rem(dy + 2, 4) + 2) + far * lax.rem(dy + 6, 8)
        return side, lax.rem(m + step, NZ)

    def piece(chip_index):
        side, block = place(chip_index)
        return pl.ds(pl.multiple_of(block * RB, RB), RB), pl.ds(pl.multiple_of(side * 256, 256), WIDE)

    def remote(src, dst, s, r, dev):
        pltpu.make_async_remote_copy(
            src_ref=src, dst_ref=dst, send_sem=s, recv_sem=r, device_id=dev, device_id_type=MESH
        ).start()

    barrier = pltpu.get_barrier_semaphore()
    beside = [lax.rem(d + 1, 2 * NCHIP), lax.rem(d + 2 * NCHIP - 1, 2 * NCHIP)]
    target = lax.rem(lax.div(d, 4) + NZ // 2, NZ)
    greet = [zdev(k) for k in (4, 3, 5, 2, 6, 1, 7)]
    greet += [(chip(k) * 2 + c, m) for k in FAR]
    greet += [sibling] + [(e, m) for e in beside]
    for dev in greet:
        pl.semaphore_signal(barrier, inc=1, device_id=dev, device_id_type=MESH)

    waits = {}

    def expect(name, buf, sem):
        waits[name] = pltpu.make_async_copy(buf, buf, sem).wait

    def settle(name):
        waits.pop(name)()

    core_tokens = pl.ds(pl.multiple_of(c * TOK, TOK), TOK)
    core_rows16 = pl.ds(pl.multiple_of(c * TB, TB), TB)
    core_rows = pl.ds(pl.multiple_of(c * HALF, HALF), HALF)
    loads = dict(
        tk=(tk_h, tk), bank=(bank_h, bank), lids=(lids_h, lids), tg=(tg_h, tg.at[core_tokens]),
        ids=(ids_h, ids), bias=(bias_h, bias), gate=(gate_h, gate),
        dw=(dw_h, dw), go=(go_h.at[core_rows], go),
    )
    number = {name: i for i, name in enumerate(loads)}

    def load(name):
        src, dst = loads[name]
        copy = pltpu.make_async_copy(src, dst, lsem.at[number[name]])
        copy.start()
        waits[name] = copy.wait

    def load_kw(ch):
        copy = pltpu.make_async_copy(kw_h.at[:, pl.ds(ch * CH, CH)], kw.at[ch], kwsem.at[ch])
        copy.start()
        waits["kw", ch] = copy.wait
        copy = pltpu.make_async_copy(gw_h.at[:, pl.ds(ch * CH, CH)], gw.at[ch], kwsem.at[NCH + ch])
        copy.start()
        waits["gw", ch] = copy.wait

    for name in ("lids", "tk", "bank", "tg", "ids", "bias", "gate"):
        load(name)

    settle("lids")
    ids_row = lids[...].astype(F32)
    rows0 = lax.broadcasted_iota(jnp.int32, (ROWS, ROWS), 0)
    rows1 = lax.broadcasted_iota(jnp.int32, (ROWS, ROWS), 1)
    ids_col = jnp.sum(
        jnp.where(rows0 == rows1, jnp.broadcast_to(ids_row, (ROWS, ROWS)), 0.0), axis=1, keepdims=True
    )
    ordered = 32 * ((rows1 >> 4) & 7) + 16 * (rows1 >> 7) + (rows1 & 15)
    ids_ordered = jnp.sum(
        jnp.where(rows0 == ordered, jnp.broadcast_to(ids_col, (ROWS, ROWS)), 0.0), axis=0, keepdims=True
    )
    pick_t = (
        lax.broadcasted_iota(jnp.int32, (BANK, ROWS), 0).astype(F32) == ids_ordered
    ).astype(F32).astype(BF16)
    load_kw(0)
    settle("tk")
    settle("tg")

    def bank_part():
        settle("bank")
        bank_scores = lax.dot_general(tk[...], bank[...], NT, preferred_element_type=F32).astype(BF16)
        pbuf[NCH] = jnp.dot(bank_scores, pick_t, preferred_element_type=F32).astype(BF16)

    bank_part()
    load_kw(1)

    def partial_sum(ch):
        settle(("kw", ch))
        settle(("gw", ch))
        if ch + 2 < NCH:
            load_kw(ch + 2)
        elif ch + 2 == NCH:
            load("dw")
        else:
            load("go")
        value = jnp.dot(tk[...], kw[ch], preferred_element_type=F32)
        value = value + jnp.dot(
            tg[core_tokens], gw[ch], preferred_element_type=F32
        )
        pbuf[ch] = value.astype(BF16)

    def send_partial(first, many):
        for far in (4, 3, 5, 2, 6, 1, 7):
            k = far + c * (NZ - 2 * far)
            to = lax.rem(m + k, NZ)
            rows = pl.ds(pl.multiple_of(to * TB, TB), TB)
            remote(
                pbuf.at[pl.ds(first, many), rows], rz.at[pl.ds(first, many), k - 1],
                rz_s.at[first], rz_r.at[first], (d, to),
            )
        expect(("rz", first), rz.at[pl.ds(first, many)], rz_r.at[first])
        expect(("rz sent", first), rz.at[pl.ds(first, many)], rz_s.at[first])

    settle("ids")
    pl.semaphore_wait(barrier, len(greet))
    send_partial(NCH, 1)
    partial_sum(0)
    send_partial(0, 1)
    remote(tg.at[core_tokens], tg.at[core_tokens], c_s.at[2], c_r.at[2], sibling)
    expect("tg other", tg.at[core_tokens], c_r.at[2])
    expect("tg sent", tg.at[core_tokens], c_s.at[2])
    for i, e in enumerate(beside):
        remote(ids, near.at[i], i_s.at[i], i_r.at[i], (e, m))
        expect(("near", i), near.at[i], i_r.at[i])
        expect(("near sent", i), near.at[i], i_s.at[i])
    for ch in range(1, NCH):
        partial_sum(ch)
        if ch == NCH - 1:
            send_partial(1, 3)

    settle("dw")
    pick = (
        lax.broadcasted_iota(jnp.int32, (ROWS, BANK), 1).astype(F32) == ids_col
    ).astype(F32).astype(BF16)
    bank_down = lax.dot_general(bank[...], dw[...], NT, preferred_element_type=F32).astype(BF16)
    bbuf[...] = jnp.dot(pick, bank_down, preferred_element_type=F32).astype(BF16)

    own_ids = ids[...].astype(F32)
    wanted = lax.broadcasted_iota(jnp.int32, (TB, TOK), 1) == (
        lax.broadcasted_iota(jnp.int32, (TB, TOK), 0) + m * TB
    )
    ids_here = jnp.sum(jnp.where(wanted, jnp.broadcast_to(own_ids, (TB, TOK)), 0.0), axis=1, keepdims=True)
    count = jnp.sum((ids_here == own_ids).astype(F32), axis=1, keepdims=True)
    for i in range(2):
        settle(("near", i))
        count = count + jnp.sum((ids_here == near[i].astype(F32)).astype(F32), axis=1, keepdims=True)

    factor[...] = jnp.broadcast_to(2.0 / count, (TB, ROWS))
    settle("bias")
    settle("gate")
    mine = pl.ds(pl.multiple_of(m * TB, TB), TB)

    def summed(ch):
        if ("rz", ch) in waits:
            settle(("rz", ch))
        value = pbuf[ch, mine].astype(F32)
        for k in range(NZ - 1):
            value = value + rz[ch, k].astype(F32)
        return value

    gated = jnp.zeros((TB, CH), F32)
    for ch in range(NCH):
        cut = slice(ch * CH, (ch + 1) * CH)
        hidden = jnp.maximum(summed(ch) + bias[:, cut], 0.0).astype(BF16)
        hid[:, cut] = hidden
        gated = gated + hidden.astype(F32) * gate[:, cut]
    weight = jax.nn.sigmoid(jnp.sum(gated, axis=1, keepdims=True)) * factor[...]
    def half(core):
        return pl.ds(pl.multiple_of(core * HALF, HALF), HALF)

    remote(hid.at[:, half(1 - c)], hid2.at[core_rows16], c_s.at[1], c_r.at[1], sibling)
    expect("hid2", hid2.at[core_rows16], c_r.at[1])
    expect("hid2 sent", hid2.at[core_rows16], c_s.at[1])
    hid2[core_rows16] = hid[:, half(c)]
    sw2[core_rows16] = (summed(NCH) * weight).astype(BF16)
    remote(sw2.at[core_rows16], sw2.at[core_rows16], c_s.at[0], c_r.at[0], sibling)
    expect("sw2", sw2.at[core_rows16], c_r.at[0])
    expect("sw2 sent", sw2.at[core_rows16], c_s.at[0])

    def lanes(core):
        return pl.ds(pl.multiple_of(core * 128, 128), 128)

    my_tokens = pl.ds(pl.multiple_of(c * TOK + m * TB, TB), TB)

    def send_scores(core, k):
        remote(
            sw2.at[core_rows16, lanes(core)], swx.at[my_tokens], a_s.at[0], a_r.at[0],
            (q * 2 + core, lax.rem(m + k, NZ)),
        )

    swx[my_tokens] = sw2[core_rows16, lanes(c)]
    for k in (4, 3, 5, 2, 6, 1, 7):
        for core in range(2):
            send_scores(core, k)
    send_scores(1 - c, 0)
    expect("swx", swx.at[pl.ds(0, 2 * TOK - TB)], a_r.at[0])
    expect("swx sent", swx.at[pl.ds(0, 2 * TOK - TB)], a_s.at[0])

    settle("hid2")
    settle("sw2")
    for part in range(2):
        units = slice(part * CH, (part + 1) * CH)
        uh_sum[part] = lax.dot_general(sw2[...], hid2[:, units], TN, preferred_element_type=F32).astype(BF16)
        for k in FAR:
            to = chip(k)
            remote(
                uh_sum.at[part, rows_of(to)], uh_rs.at[part, k - 1], x_s.at[part], x_r.at[part], (to * 2 + c, m)
            )
        expect(("uh_rs", part), uh_rs.at[part], x_r.at[part])
        expect(("uh_rs sent", part), uh_rs.at[part], x_s.at[part])

    for k in range(1, NZ):
        to = lax.rem(m + k, NZ)
        remote(
            bbuf.at[pl.ds(pl.multiple_of(to * OB, OB), OB)], br.at[k - 1], b_s.at[0], b_r.at[0], (d, to)
        )
    expect("br", br, b_r.at[0])
    expect("br sent", br, b_s.at[0])

    settle("tg other")
    settle("swx")
    ug_sum[...] = lax.dot_general(swx[...], tg[...], TN, preferred_element_type=F32).astype(BF16)
    for k in FAR:
        to = chip(k)
        remote(ug_sum.at[piece(to)], ug_rs.at[k - 1], x_s.at[2], x_r.at[2], (to * 2 + c, m))
    expect("ug_rs", ug_rs, x_r.at[2])
    expect("ug_rs sent", ug_rs, x_s.at[2])

    plane = []
    for part in range(2):
        settle(("uh_rs", part))
        value = uh_sum[part, rows_of(q)].astype(F32)
        for k in range(NCHIP - 1):
            value = value + uh_rs[part, k].astype(F32)
        plane.append(value)
        uz_tx[part] = value.astype(BF16)
        for far in (4, 3, 5, 2, 6, 1, 7):
            k = far + c * (NZ - 2 * far)
            remote(uz_tx.at[part], uz.at[part, k - 1], z_s.at[part], z_r.at[part], zdev(k))
        expect(("uz", part), uz.at[part], z_r.at[part])
        expect(("uz sent", part), uz.at[part], z_s.at[part])

    settle("go")
    product = jnp.zeros((RB, GRADS), F32)
    for part in range(2):
        settle(("uz", part))
        value = plane[part]
        for k in range(NZ - 1):
            value = value + uz[part, k].astype(F32)
        product = product + jnp.dot(
            value.astype(BF16), go[part * CH:(part + 1) * CH], preferred_element_type=F32
        )
    ftx[...] = product.astype(BF16)
    slot = lax.rem(d, 4)
    for j in range(4):
        remote(ftx.at[:, pl.ds(128 * j, 256)], frx.at[slot], f_s.at[0], f_r.at[0], (4 * m + j, target))
    expect("frx", frx, f_r.at[0])
    expect("frx sent", frx, f_s.at[0])

    settle("ug_rs")
    grads_part = ug_sum[piece(q)].astype(F32)
    for k in range(NCHIP - 1):
        grads_part = grads_part + ug_rs[k].astype(F32)
    gtx[...] = grads_part.astype(BF16)
    side, block = place(q)
    for j in range(2):
        remote(
            gtx.at[:, pl.ds(128 * j, 256)], grx.at[c], g_s.at[0], g_r.at[0], (4 * m + 2 * side + j, block)
        )
    expect("grx", grx, g_r.at[0])
    expect("grx sent", grx, g_s.at[0])

    settle("br")
    base = bbuf[pl.ds(pl.multiple_of(m * OB, OB), OB)].astype(F32)
    for k in range(NZ - 1):
        base = base + br[k].astype(F32)
    settle("grx")
    settle("frx")
    spread = jnp.concatenate(
        [
            frx[0].astype(F32) + frx[1].astype(F32) + grx[0].astype(F32),
            frx[2].astype(F32) + frx[3].astype(F32) + grx[1].astype(F32),
        ],
        axis=0,
    )
    spread = pltpu.roll(spread, lax.rem(256 - 32 * slot, 256), 1)
    out_ref[...] = (base + SCALE * spread[:, :COLS]).astype(BF16)

    for name in list(waits):
        settle(name)


def local(
    token_keys, token_grads, prompt_ids, key_weight, grad_weight, hidden_bias, gate_vector, grad_output,
    down_weight, locality_bank, locality_ids,
):
    vm = pltpu.VMEM
    dma = pltpu.SemaphoreType.DMA
    scratch = [
        vm((TOK, KEYS), BF16), vm((2 * TOK, GRADS), BF16), vm((1, TOK), jnp.int32),
        vm((NCH, KEYS, CH), BF16), vm((NCH, GRADS, CH), BF16), vm((1, HID), F32), vm((1, HID), F32),
        vm((HALF, GRADS), BF16), vm((COLS, KEYS), BF16), vm((BANK, KEYS), BF16), vm((1, ROWS), jnp.int32),
        vm((2, 1, TOK), jnp.int32), vm((TB, ROWS), F32),
        vm((NCH + 1, TOK, CH), BF16), vm((NCH + 1, NZ - 1, TB, CH), BF16),
        vm((ROWS, COLS), BF16), vm((NZ - 1, OB, COLS), BF16),
        vm((TB, HID), BF16), vm((2 * TB, ROWS), BF16), vm((2 * TB, HALF), BF16), vm((2 * TOK, 128), BF16),
        vm((2, ROWS, CH), BF16), vm((2, NCHIP - 1, RB, CH), BF16),
        vm((ROWS // 2, GRADS), BF16), vm((NCHIP - 1, RB, WIDE), BF16),
        vm((2, RB, CH), BF16), vm((2, NZ - 1, RB, CH), BF16),
        vm((RB, GRADS), BF16), vm((4, RB, 256), BF16), vm((RB, WIDE), BF16), vm((2, RB, 256), BF16),
        dma((10,)), dma((2 * NCH,)), dma((NCH + 1,)), dma((NCH + 1,)), dma((1,)), dma((1,)), dma((2,)), dma((2,)),
        dma((1,)), dma((1,)), dma((3,)), dma((3,)), dma((3,)), dma((3,)), dma((2,)), dma((2,)), dma((1,)), dma((1,)),
        dma((1,)), dma((1,)),
    ]
    any_spec = pl.BlockSpec(memory_space=pl.ANY)
    return pl.pallas_call(
        kernel,
        out_shape=pltpu.VMEM((OB, COLS), BF16),
        in_specs=[any_spec] * 11,
        out_specs=pl.BlockSpec(memory_space=pltpu.VMEM),
        scratch_shapes=scratch,
        compiler_params=pltpu.CompilerParams(
            collective_id=0, has_side_effects=True, vmem_limit_bytes=60 * 1024 * 1024
        ),
        cost_estimate=pl.CostEstimate(flops=2_000_000_000, bytes_accessed=14_000_000, transcendentals=16),
    )(
        token_keys, token_grads, prompt_ids.reshape(1, TOK), key_weight, grad_weight,
        hidden_bias.reshape(1, HID), gate_vector.reshape(1, HID), grad_output, down_weight.T, locality_bank,
        locality_ids.reshape(1, ROWS),
    )


def solution(mesh):
    placed = (
        P("dp", "mp"), P("dp", "mp"), P("dp"), P("mp", None), P("mp", None), P(), P(), P(None, "mp"),
        P("mp", "dp"), P(None, "mp"), P(),
    )
    return jax.shard_map(
        local, mesh=mesh, in_specs=placed, out_specs=P("mp", "dp"), check_vma=False
    )
```
